128 devices in a mesh: group: 8 (over x, core), tp: 16 (over y, z).
Axes of the slice: x: 4, y: 4, z: 4, core: 2. Of those that a mesh axis runs over, the one named last changes fastest.
Arguments:
- prefill_in: bfloat16 [4096, 8192], P('group', 'tp'), may hold values from -6 to 6
- decode_in: bfloat16 [2, 128, 8192], P(None, 'group', 'tp'), may hold values from -6 to 6
- norm_gain: bfloat16 [8192], replicated, may hold values from 0.25 to 1.75
- query_weight: bfloat16 [8192, 8192], P(None, 'tp'), may hold values from -0.0625 to 0.0625
- query_bias: bfloat16 [8192], P('tp'), may hold values from -8 to 8
- keyval_weight: bfloat16 [8192, 2, 1024], P(None, None, 'tp'), may hold values from -0.0625 to 0.0625
- keyval_bias: bfloat16 [2, 1024], P(None, 'tp'), may hold values from -8 to 8
- out_weight: bfloat16 [8192, 8192], P('tp'), may hold values from -0.0625 to 0.0625
- pass_offset: int32 [8], P('group'), may hold values from 0 to 4095
- routing: int32 [256, 1], P('group'), may hold values from 0 to 7; in each aligned block of 32 rows (0 to 31, 32 to 63, ...) at most 8 rows name the same one
- cache_len: int32 [128], P('group'), may hold values from 1 to 256, as said below
- page_table: int32 [128, 8], P('group'), may hold values from 0 to 63
- cache_keyval: bfloat16 [128, 256, 2, 1024], P('group', None, None, 'tp'), may hold values from -6 to 6
Outputs:
- prefill_out: bfloat16 [4096, 8192], P('group', 'tp')
- decode_out: bfloat16 [2, 128, 8192], P(None, 'group', 'tp')
The draws below stay inside these ranges and needn't reach their ends.
Inputs may be any that keep to these rules, and one draw needn't show every extreme that they name: `routing`: among the blocks of one group (aligned blocks of 32 rows) no group is named more than 8 times, a bound that some block reaches. `cache_len`: the first row of each group of 16 rows has length 256.
All inputs are finite; a program needn't handle non-finite values.
Results may differ from the reference program's by a relative error of at most 0.015.
Values may be sent and summed in bfloat16 or wider, within the bound.
A program may use at most 128 MiB of HBM per device.

```python
import math
import jax
import jax.numpy as jnp
import numpy as np
from jax import lax

D = 8192
HEADS = 64
KVH = 8
HD = 128
PASS_LEN = 512
PASSES = 1
BLK = 16
ROWS_DEV = 16
CACHE = 256
NPG = 8
STEPS = 2
NB = 32
CAP = 8
POOL = 64
TOKENS_PRE = 4096
ROWS = 128
N_GROUP = 8
N_TP = 16


def draw_query_bias(key, part):
    key = jax.random.fold_in(key, 11)
    noise = jax.random.uniform(key, (HEADS, HD), jnp.float32, -1.0, 1.0)
    values = 0.5 * noise
    return values.reshape(HEADS * HD).astype(jnp.bfloat16)


def draw_keyval_bias(key, part):
    key = jax.random.fold_in(key, 12)
    noise = jax.random.uniform(key, (2, KVH, HD), jnp.float32, -1.0, 1.0)
    key_part = 0.5 * noise[0]
    values = jnp.stack([key_part, 0.5 * noise[1]], axis=0)
    return values.reshape(2, KVH * HD).astype(jnp.bfloat16)


def draw_cache_len(key, part):
    key = jax.random.fold_in(key, 13)
    lengths = jax.random.randint(key, (ROWS,), 1, CACHE + 1, dtype=jnp.int32)
    first_rows = jnp.arange(ROWS, dtype=jnp.int32) % ROWS_DEV == 0
    return jnp.where(first_rows, CACHE, lengths).astype(jnp.int32)


def with_ends(values, rng, smallest, high):
    dims = values.shape
    place = [jax.random.randint(jax.random.fold_in(rng, axis), (), 0, dims[axis]) for axis in range(len(dims))]
    values = values.at[tuple(place)].set(smallest)
    longest = dims.index(max(dims))
    place[longest] = (place[longest] + 1) % dims[longest]
    return values.at[tuple(place)].set(high)


def levels(stream_key, extent, shards, smallest, high):
    loudness, own = 1.0, jax.random.fold_in(stream_key, 6)
    for axis_at, shards_of in shards:
        steps = jnp.exp(jax.random.uniform(jax.random.fold_in(own, axis_at), (shards_of,), jnp.float32, smallest / len(shards), high / len(shards)))
        loudness = loudness * jnp.repeat(steps, extent[axis_at] // shards_of).reshape([-1 if axis == axis_at else 1 for axis in range(len(extent))])
    return loudness


def routed_block(key, own, number, rows, number_of, top, reach, skew):
    sequence = jax.random.permutation(key, number_of)
    crowded, ordinary = portions_of(number_of, rows * top, reach, skew, True), portions_of(number_of, rows * top, reach, skew, False)
    places = jnp.arange(number_of)

    def named(tallies, offset_by):
        used = int((tallies > 0).sum())
        fixed = max(1, used // 4)
        moved = fixed + (places - fixed + offset_by * (used - fixed)) % max(1, number_of - fixed)
        return jnp.zeros((number_of,), jnp.int32).at[sequence[jnp.where(places < fixed, places, moved)]].set(jnp.asarray(tallies, jnp.int32))

    tallies = jnp.where(number % 4 == 0, named(crowded, number // 4), named(ordinary, number - number // 4 - 1))
    mixed = jax.random.permutation(jax.random.fold_in(own, 3), number_of)
    giver, receiver = mixed[0:number_of // 2 * 2:2], mixed[1:number_of // 2 * 2:2]
    slack = jnp.minimum(tallies[giver] - 1, reach - tallies[receiver]) // 2
    slack = jnp.where((giver == sequence[0]) | (receiver == sequence[0]) | (tallies[receiver] == 0), 0, jnp.maximum(slack, 0))
    moved = jax.random.randint(jax.random.fold_in(own, 4), (number_of // 2,), 0, 1 << 20) % (slack + 1)
    tallies = tallies.at[giver].add(-moved).at[receiver].add(moved)
    labels = jnp.searchsorted(jnp.cumsum(tallies), jnp.arange(rows * top), side="right").astype(jnp.int32)
    listing = labels.reshape(top, rows).T
    listing = listing[jax.random.permutation(jax.random.fold_in(own, 1), rows)]
    offset_by = jax.random.randint(jax.random.fold_in(own, 2), (rows, 1), 0, top)
    return jnp.take_along_axis(listing, (jnp.arange(top)[None, :] + offset_by) % top, axis=1)


def portions_of(count, total, most, slope, full):
    weights = [(1 << 20) // math.isqrt(standing ** slope) + 1 for standing in range(1, count + 1)]
    largest = most if full else min(most, max(-(-total // count), total * weights[0] // sum(weights)))
    least = 1 if total - largest >= count - 1 else 0
    given, surplus = [largest] + [least] * (count - 1), total - largest - least * (count - 1)
    while surplus > 0:
        movable = [i for i in range(1, count) if given[i] < largest] or [i for i in range(1, count) if given[i] < most]
        whole, left = sum([weights[i] for i in movable]), surplus
        for i in movable:
            more = min(most - given[i], max(1, left * weights[i] // whole), surplus)
            given[i] = given[i] + more
            surplus = surplus - more
    return np.array(given)


def gaussian(key, extent, deviation, limit, cuts=(), held_as=jnp.bfloat16):
    entries = deviation * jax.random.normal(key, extent, jnp.float32)
    if cuts:
        entries = entries * levels(key, extent, cuts, -0.22, 0.18)
    return jnp.clip(entries, -limit, limit).astype(held_as)


def setup_inputs(seed: int = 0) -> dict:
    key_of = jax.random.split(jax.random.key(seed), 14)
    prefill_in = gaussian(key_of[0], (TOKENS_PRE, D), 1.0, 6.0, ((0, 8), (1, 16)))
    decode_in = gaussian(key_of[1], (STEPS, ROWS, D), 1.0, 6.0, ((1, 8), (2, 16)))
    norm_gain = jnp.clip(1.0 + 0.15 * jax.random.normal(key_of[2], (D,), jnp.float32), 0.25, 1.75).astype(jnp.bfloat16)
    query_weight = gaussian(key_of[3], (D, HEADS * HD), D ** -0.5, 0.0625, ((1, 16),))
    query_bias = draw_query_bias(jax.random.fold_in(key_of[13], 71), 0)
    keyval_weight = gaussian(key_of[5], (D, 2, KVH * HD), D ** -0.5, 0.0625, ((2, 16),))
    keyval_bias = draw_keyval_bias(jax.random.fold_in(key_of[13], 71), 0)
    out_weight = gaussian(key_of[7], (HEADS * HD, D), (HEADS * HD) ** -0.5, 0.0625, ((0, 16),))
    pass_offset = with_ends(jax.random.randint(key_of[8], (N_GROUP * PASSES,), 0, 4096), jax.random.fold_in(key_of[8], 1), 0, 4095).astype(jnp.int32)
    routing_keys = jax.random.split(jax.random.fold_in(key_of[9], 1), (N_GROUP * NB) // NB)
    routing_turns = jax.random.permutation(jax.random.fold_in(key_of[9], 3), (N_GROUP * NB) // NB)
    routing = jax.vmap(lambda own, number: routed_block(jax.random.fold_in(key_of[9], 2), own, number, NB, N_GROUP, 1, CAP, 2))(routing_keys, routing_turns).reshape((N_GROUP * NB, 1))
    cache_len = draw_cache_len(jax.random.fold_in(key_of[13], 71), 0)
    page_table = with_ends(jax.random.randint(key_of[11], (ROWS, NPG), 0, POOL), jax.random.fold_in(key_of[11], 1), 0, POOL - 1).astype(jnp.int32)
    cache_keyval = gaussian(key_of[12], (ROWS, CACHE, 2, KVH * HD), 1.0, 6.0, ((0, 8), (3, 16)))
    return {"prefill_in": prefill_in, "decode_in": decode_in, "norm_gain": norm_gain, "query_weight": query_weight, "query_bias": query_bias, "keyval_weight": keyval_weight, "keyval_bias": keyval_bias, "out_weight": out_weight, "pass_offset": pass_offset, "routing": routing, "cache_len": cache_len, "page_table": page_table, "cache_keyval": cache_keyval}


NEG_FILL = -1e+30
EPSILON = 1e-06

def normalize(values, norm_gain):
    widened = values.astype(jnp.float32)
    mean_square = lax.optimization_barrier(jnp.mean(widened * widened, axis=-1, keepdims=True))
    return (widened * lax.rsqrt(mean_square + EPSILON) * norm_gain.astype(jnp.float32)).astype(jnp.bfloat16)

def rotate(heads_in, places):
    half_size = heads_in.shape[-1] // 2
    frequencies = 1000000.0 ** (-(jnp.arange(half_size, dtype=jnp.float32) * (2.0 / heads_in.shape[-1])))
    angles = places[..., None, None] * frequencies
    cosine = jnp.cos(angles)
    sine_part = jnp.sin(angles)
    widened = heads_in.astype(jnp.float32)
    lower_half = widened[..., :half_size]
    upper_half = widened[..., half_size:]
    return jnp.concatenate([lower_half * cosine - upper_half * sine_part, upper_half * cosine + lower_half * sine_part], axis=-1)

def softmax_rounded(scores):
    largest = lax.optimization_barrier(jnp.max(scores, axis=-1, keepdims=True))
    raised = jnp.exp(scores - largest)
    return (raised / lax.optimization_barrier(jnp.sum(raised, axis=-1, keepdims=True))).astype(jnp.bfloat16)

def head_sum(attended, out_weight, residual):
    width = attended.shape[1] // N_TP

    def add_share(index, total):
        start = (index * width).astype(jnp.int32)
        piece = lax.dynamic_slice_in_dim(attended, start, width, 1)
        rows_part = lax.dynamic_slice_in_dim(out_weight, start, width, 0)
        share = jnp.dot(piece, rows_part, preferred_element_type=jnp.float32).astype(jnp.bfloat16)
        share = lax.optimization_barrier(share)
        return total + share.astype(jnp.float32)
    total = lax.fori_loop(0, N_TP, add_share, jnp.zeros((attended.shape[0], out_weight.shape[1]), jnp.float32))
    return (residual.astype(jnp.float32) + total).astype(jnp.bfloat16)

def reference(prefill_in, decode_in, norm_gain, query_weight, query_bias, keyval_weight, keyval_bias, out_weight, pass_offset, routing, cache_len, page_table, cache_keyval):
    scale = HD ** (-0.5)
    group_size = HEADS // KVH
    token_count = prefill_in.shape[0]
    keyval_flat = keyval_weight.reshape(D, 2 * KVH * HD)
    keyval_add = keyval_bias.reshape(2 * KVH * HD).astype(jnp.float32)
    normed = normalize(prefill_in, norm_gain)
    queries = jnp.dot(normed, query_weight, preferred_element_type=jnp.float32) + query_bias.astype(jnp.float32)
    keyval = (jnp.dot(normed, keyval_flat, preferred_element_type=jnp.float32) + keyval_add).astype(jnp.bfloat16)
    keyval = keyval.reshape(token_count, 2, KVH, HD)
    places = (jnp.repeat(pass_offset, PASS_LEN) + jnp.tile(jnp.arange(PASS_LEN, dtype=jnp.int32), N_GROUP * PASSES)).astype(jnp.float32)
    query_rot = rotate(queries.reshape(token_count, HEADS, HD), places).astype(jnp.bfloat16)
    key_rot = rotate(keyval[:, 0], places).astype(jnp.bfloat16)
    values_new = keyval[:, 1]
    causal = jnp.arange(PASS_LEN)[:, None] >= jnp.arange(PASS_LEN)[None, :]

    def attend_pass(pieces):
        query_part, key_part, value_part = pieces
        grouped = query_part.reshape(PASS_LEN, KVH, group_size, HD).astype(jnp.float32)
        scores = jnp.einsum('qkgd,tkd->kgqt', grouped, key_part.astype(jnp.float32)) * scale
        weights = softmax_rounded(jnp.where(causal, scores, NEG_FILL))
        mixed = jnp.einsum('kgqt,tkd->qkgd', weights.astype(jnp.float32), value_part.astype(jnp.float32))
        return mixed.reshape(PASS_LEN, HEADS * HD).astype(jnp.bfloat16)
    pass_count = token_count // PASS_LEN
    attended = lax.map(attend_pass, (query_rot.reshape(pass_count, PASS_LEN, HEADS, HD), key_rot.reshape(pass_count, PASS_LEN, KVH, HD), values_new.reshape(pass_count, PASS_LEN, KVH, HD)))
    attended = attended.reshape(token_count, HEADS * HD)
    prefill_out = head_sum(attended, out_weight, prefill_in)
    stored = jnp.stack([key_rot, values_new], axis=1).reshape(N_GROUP, NB, BLK * 2 * KVH * HD)
    destination = routing[:, 0].reshape(N_GROUP, NB)
    group_iota = jnp.arange(N_GROUP, dtype=jnp.int32)
    marks = (destination[:, :, None] == group_iota[None, None, :]).astype(jnp.int32)
    ranks = lax.optimization_barrier(jnp.sum((jnp.cumsum(marks, axis=1) - marks) * marks, axis=-1))
    chosen = (destination[None, :, None, :] == group_iota[:, None, None, None]) & (ranks[None, :, None, :] == jnp.arange(CAP, dtype=jnp.int32)[None, None, :, None])
    chosen = chosen.astype(jnp.float32)
    pool = jnp.einsum('dscb,sbx->dscx', chosen, stored.astype(jnp.float32)).astype(jnp.bfloat16)
    pool = pool.reshape(N_GROUP, POOL, BLK, 2, KVH, HD)
    filled = lax.optimization_barrier(jnp.sum(chosen, axis=-1)).reshape(N_GROUP, POOL) > 0.5
    steps_rows = STEPS * ROWS
    normed_dec = normalize(decode_in, norm_gain).reshape(steps_rows, D)
    queries_dec = (jnp.dot(normed_dec, query_weight, preferred_element_type=jnp.float32) + query_bias.astype(jnp.float32)).reshape(STEPS, ROWS, HEADS, HD)
    keyval_dec = (jnp.dot(normed_dec, keyval_flat, preferred_element_type=jnp.float32) + keyval_add).astype(jnp.bfloat16)
    keyval_dec = keyval_dec.reshape(STEPS, ROWS, 2, KVH, HD)
    places_dec = (cache_len[None, :] + jnp.arange(STEPS, dtype=jnp.int32)[:, None]).astype(jnp.float32)
    query_dec = rotate(queries_dec, places_dec).astype(jnp.bfloat16)
    key_dec = rotate(keyval_dec[:, :, 0], places_dec).astype(jnp.bfloat16)
    value_dec = keyval_dec[:, :, 1]
    owner = jnp.arange(ROWS, dtype=jnp.int32) // ROWS_DEV
    pages = pool[owner[:, None], page_table].reshape(ROWS, NPG * BLK, 2, KVH, HD)
    page_ok = jnp.repeat(filled[owner[:, None], page_table], BLK, axis=1)
    cache_ok = jnp.arange(CACHE, dtype=jnp.int32)[None, :] < cache_len[:, None]
    history = jnp.concatenate([cache_keyval.reshape(ROWS, CACHE, 2, KVH, HD), pages], axis=1)
    visible = jnp.concatenate([cache_ok, page_ok], axis=1)
    earlier = jnp.arange(STEPS)[None, :] <= jnp.arange(STEPS)[:, None]

    def attend_row(pieces):
        query_row, history_row, seen_row, key_row, value_row = pieces
        grouped = query_row.reshape(STEPS, KVH, group_size, HD).astype(jnp.float32)
        old_scores = jnp.einsum('skgd,mkd->skgm', grouped, history_row[:, 0].astype(jnp.float32)) * scale
        old_scores = jnp.where(seen_row[None, None, None, :], old_scores, NEG_FILL)
        new_scores = jnp.einsum('skgd,jkd->skgj', grouped, key_row.astype(jnp.float32)) * scale
        new_scores = jnp.where(earlier[:, None, None, :], new_scores, NEG_FILL)
        weights = softmax_rounded(jnp.concatenate([old_scores, new_scores], axis=-1)).astype(jnp.float32)
        span = history_row.shape[0]
        mixed = jnp.einsum('skgm,mkd->skgd', weights[..., :span], history_row[:, 1].astype(jnp.float32))
        mixed = mixed + jnp.einsum('skgj,jkd->skgd', weights[..., span:], value_row.astype(jnp.float32))
        return mixed.reshape(STEPS, HEADS * HD).astype(jnp.bfloat16)
    attended_dec = lax.map(attend_row, (query_dec.transpose(1, 0, 2, 3), history, visible, key_dec.transpose(1, 0, 2, 3), value_dec.transpose(1, 0, 2, 3)))
    attended_dec = attended_dec.transpose(1, 0, 2).reshape(steps_rows, HEADS * HD)
    decode_out = head_sum(attended_dec, out_weight, decode_in.reshape(steps_rows, D)).reshape(STEPS, ROWS, D)
    return (prefill_out, decode_out)
```

```python
import jax
import jax.numpy as jnp
import numpy as np
from jax import lax
from jax.experimental import pallas as pl
from jax.experimental.pallas import tpu as pltpu
from jax.sharding import PartitionSpec as P

MESH = pl.DeviceIdType.MESH
F32 = jnp.float32
BF16 = jnp.bfloat16
HD = 128
FS = 512
C0, C1 = 288, 256
DEC = 32
NEG_FILL = -1e30
EPSILON = 1e-06
CACHE = 256
WIDTH = 8192


def nt(a, b):
    return lax.dot_general(a, b, (((1,), (1,)), ((), ())), preferred_element_type=F32)


def mm(a, b):
    return jnp.dot(a, b, preferred_element_type=F32)


def offset_of(k):
    return k + k // 2 - 2 * (k // 3)


def kernel(
    pre_in, dec_in, gain, qbias, kvbias, freq, offset, routing, lens, table,
    wq_hbm, wkv_hbm, wo_hbm, cache_hbm,
    pre_out, dec_out,
    x0, x1, wq, wkv, wo, acc0, acc1, ss0, ss1, cos_t, sin_t,
    q0, q1, kvs0, kvs1, kvr0, kvr1, kv, kvd, att0, att1, attd,
    cache_own, cache_other, pack, pool, cnt_s, cnt_r, qx, ox_s, ox_r, mult,
    tok_slot,
    rs0, rs1, rsd,
    w_sem, ag_send, ag_recv, rs_send, rs_recv, pair_send, pair_recv, grp_send, grp_recv,
):
    g = lax.axis_index("group")
    t = lax.axis_index("tp")
    core = g % 2
    y, z = t // 4, t % 4
    f = z + core * (y - z)
    s = y + core * (z - y)

    def tp_of(ff, ss):
        return 4 * ss + ff + core * 3 * (ff - ss)

    fn, fp = tp_of((f + 1) % 4, s), tp_of((f + 3) % 4, s)
    sn, sp = tp_of(f, (s + 1) % 4), tp_of(f, (s + 3) % 4)
    pair = t + 1 - 2 * (t % 2)
    half = t % 2

    drows = dec_in[...].astype(F32)
    drows = jnp.concatenate([drows[0:8], drows[16:24], drows[8:16], drows[24:32]], axis=0)
    first = jnp.concatenate([drows.astype(BF16), pre_in[0:256]], axis=0)
    x0[0] = first.reshape(2, C0 // 2, FS)
    x1[0] = pre_in[256:512].reshape(2, C1 // 2, FS)

    barrier = pltpu.get_barrier_semaphore()
    for peer in (fn, fp, sn, sp):
        pl.semaphore_signal(barrier, inc=1, device_id=(g, peer), device_id_type=MESH)
    for j in range(1, 8):
        pl.semaphore_signal(barrier, inc=1, device_id=((g + j) % 8, t), device_id_type=MESH)

    loads = [
        pltpu.make_async_copy(wq_hbm, wq, w_sem.at[0]),
        pltpu.make_async_copy(wkv_hbm, wkv, w_sem.at[1]),
        pltpu.make_async_copy(wo_hbm, wo, w_sem.at[2]),
        pltpu.make_async_copy(cache_hbm.at[pl.ds(8 * half, 8)], cache_own, w_sem.at[3]),
    ]
    for load in loads:
        load.start()

    pl.semaphore_wait(barrier, 11)

    def to_tp(src, dst, send, recv, peer):
        return pltpu.make_async_remote_copy(src, dst, send, recv, device_id=(g, peer), device_id_type=MESH)

    class Gather:
        def __init__(self, x, rows, c):
            self.x, self.c, self.sent = x, c, []

        def copy(self, src, dst, part, index, peer):
            src, dst = 4 * src[0] + src[1], 4 * dst[0] + dst[1]
            src = self.x.at[src] if part is None else self.x.at[src, part]
            dst = self.x.at[dst] if part is None else self.x.at[dst, part]
            return to_tp(src, dst, ag_send.at[self.c, index], ag_recv.at[self.c, index], peer)

        def go(self, src, dst, part, index, peer):
            copy = self.copy(src, dst, part, index, peer)
            copy.start()
            self.sent.append(copy)

        def came(self, dst, part, index):
            self.copy(dst, dst, part, index, fn).wait_recv()

        def send_own(self):
            self.go((0, 0), (2, 0), None, 0, fn)
            self.go((0, 0), (1, 0), None, 1, fp)
            self.line(0)

        def line(self, k):
            self.go((k, 0), (k, 2), None, 4 + 4 * k, sn)
            self.go((k, 0), (k, 1), None, 5 + 4 * k, sp)

        def near(self):
            self.came((2, 0), None, 0)
            self.go((2, 0), (3, 0), 0, 2, fn)
            self.line(2)
            self.came((1, 0), None, 1)
            self.go((1, 0), (3, 0), 1, 3, fp)
            self.line(1)

        def far(self):
            self.came((3, 0), 0, 2)
            self.came((3, 0), 1, 3)
            self.line(3)

        def step(self, i):
            j, w = (i - 3) // 3, (i - 3) % 3
            if i < 3:
                if i == 1:
                    self.near()
                return i, 0
            if i == 5:
                self.far()
                return 3, 0
            if i == 15 or w == 2:
                self.came((j - 1, 3), 0, 2 + 4 * j)
                self.came((j - 1, 3), 1, 3 + 4 * j)
                return j - 1, 3
            if w == 0:
                self.came((j, 2), None, 4 + 4 * j)
                self.go((j, 2), (j, 3), 0, 6 + 4 * j, sn)
                return j, 2
            self.came((j, 1), None, 5 + 4 * j)
            self.go((j, 1), (j, 3), 1, 7 + 4 * j, sp)
            return j, 1

        def drain(self):
            for copy in self.sent:
                copy.wait_send()

    ag0, ag1 = Gather(x0, C0, 0), Gather(x1, C1, 1)
    ag0.send_own()

    def accumulate(x, acc, ss, place):
        kf, ks = place
        at = pl.multiple_of(tp_of((f + offset_of(kf)) % 4, (s + offset_of(ks)) % 4) * FS, FS)
        xf = x[4 * kf + ks].reshape(-1, FS).astype(F32)
        sq = xf * xf
        ss[...] += sq[:, 0:128] + sq[:, 128:256] + sq[:, 256:384] + sq[:, 384:512]
        xg = (xf * gain[:, pl.ds(at, FS)].astype(F32)).astype(BF16)
        acc[:, 0:512] += mm(xg, wq[pl.ds(at, FS), :])
        acc[:, 512:640] += nt(xg, wkv[:, pl.ds(at, FS)])

    lane = lax.broadcasted_iota(jnp.int32, (C0, HD), 1)
    row = lax.broadcasted_iota(jnp.int32, (C0, HD), 0)
    places = row - DEC + offset[0]
    for r in range(16):
        base = (r // 8) * 16 + r % 8
        places = jnp.where(row == base, lens[r], places)
        places = jnp.where(row == base + 8, lens[r] + 1, places)
    sign = jnp.where(lane < 64, -1.0, 1.0).astype(F32)
    angle = places.astype(F32) * freq[...]
    cos_t[0:C0] = jnp.cos(angle)
    sin_t[0:C0] = jnp.sin(angle) * sign
    angle = (row[0:C1] + (C1 + offset[0])).astype(F32) * freq[...]
    cos_t[C0:C0 + C1] = jnp.cos(angle)
    sin_t[C0:C0 + C1] = jnp.sin(angle) * sign[0:C1]

    token = lax.broadcasted_iota(jnp.int32, (8, 512), 1)

    def rank_block(b, carry):
        slots, counts = carry
        d = routing[b]
        rank = jnp.int32(0)
        for k in range(8):
            rank = rank + jnp.where(d == k, counts[k], 0)
        slots = jnp.where(token // 16 == b, d * 128 + rank * 16 + token % 16, slots)
        return slots, tuple(counts[k] + jnp.where(d == k, 1, 0) for k in range(8))

    slots, counts = lax.fori_loop(
        0, 32, rank_block, (jnp.zeros((8, 512), jnp.int32), (jnp.int32(0),) * 8)
    )
    tok_slot[...] = slots
    for k in range(8):
        cnt_s[k] = jnp.full((8, 128), 1.0, F32) * counts[k].astype(F32)

    page = lax.broadcasted_iota(jnp.int32, (8, 1024), 1) // 16
    prow = lax.broadcasted_iota(jnp.int32, (8, 1024), 0)

    def count_pages(i, times):
        r, j = i // 8, i % 8
        return times + jnp.where((prow == r) & (page == table[j, half * 8 + r]), 1.0, 0.0)

    mult[...] = lax.fori_loop(0, 64, count_pages, jnp.zeros((8, 1024), F32))

    acc0[...] = jnp.zeros_like(acc0)
    acc1[...] = jnp.zeros_like(acc1)
    ss0[...] = jnp.zeros_like(ss0)
    ss1[...] = jnp.zeros_like(ss1)
    loads[0].wait()
    loads[1].wait()

    for i in range(16):
        slot = ag0.step(i)
        if i == 1:
            ag1.send_own()
        accumulate(x0, acc0, ss0, slot)

    def finish(acc, ss, kvs, q, table_at, rows):
        inv = lax.rsqrt(jnp.sum(ss[...], axis=1, keepdims=True) * (1.0 / WIDTH) + EPSILON)
        kvs[...] = (acc[:, 512:640] * inv + kvbias[...].astype(F32)).astype(BF16)
        return inv

    def finish_q(acc, ss, q, table_at, rows):
        inv = lax.rsqrt(jnp.sum(ss[...], axis=1, keepdims=True) * (1.0 / WIDTH) + EPSILON)
        c, sn_ = cos_t[table_at:table_at + rows], sin_t[table_at:table_at + rows]
        for h in range(4):
            at = slice(h * HD, (h + 1) * HD)
            v = acc[:, at] * inv + qbias[:, at].astype(F32)
            q[:, at] = (v * c + pltpu.roll(v, 64, 1) * sn_).astype(BF16)

    def join(own, other, table_at, rows):
        a, b = own[...].astype(F32), other[...].astype(F32)
        lo = jnp.where(half == 0, a, b)
        hi = jnp.where(half == 0, b, a)
        low = lax.broadcasted_iota(jnp.int32, (rows, HD), 1) < 64
        k = jnp.where(low, lo, pltpu.roll(hi, 64, 1))
        v = jnp.where(low, pltpu.roll(lo, 64, 1), hi)
        k = k * cos_t[table_at:table_at + rows] + pltpu.roll(k, 64, 1) * sin_t[table_at:table_at + rows]
        return k.astype(BF16), v.astype(BF16)

    def pair_copy(src, dst, index):
        return to_tp(src, dst, pair_send.at[index], pair_recv.at[index], pair)

    kv_join = [pair_copy(kvs0, kvr0, 0), pair_copy(kvs1, kvr1, 1)]
    q_swap = pair_copy(q0.at[pl.ds(pl.multiple_of((1 - half) * 16, 16), 16)], qx, 2)
    cache_swap = pair_copy(cache_hbm.at[pl.ds(8 * (1 - half), 8)], cache_other, 3)
    o_swap = pair_copy(ox_s, ox_r, 4)

    scale = HD ** (-0.5)

    def attend(q, start, att, h, keys):
        at = pl.ds(h * HD, HD)
        sc = nt(q[start:start + 256, at], kv[0:keys, 0:HD]) * scale
        qi = lax.broadcasted_iota(jnp.int32, (256, keys), 0) + (keys - 256)
        ki = lax.broadcasted_iota(jnp.int32, (256, keys), 1)
        sc = jnp.where(ki <= qi, sc, NEG_FILL)
        e = jnp.exp(sc - jnp.max(sc, axis=1, keepdims=True))
        total = jnp.sum(e, axis=1, keepdims=True)
        att[:, at] = (mm(e.astype(BF16), kv[0:keys, HD:2 * HD]) / total).astype(BF16)

    for i in range(16):
        slot = ag1.step(i)
        if i == 2:
            finish(acc0, ss0, kvs0, q0, 0, C0)
            kv_join[0].start()
            finish_q(acc0, ss0, q0, 0, C0)
            q_swap.start()
        if i == 4:
            kv_join[0].wait_recv()
            k, v = join(kvs0, kvr0, 0, C0)
            kvd[:, 0:HD] = k[0:DEC]
            kvd[:, HD:2 * HD] = v[0:DEC]
            kv[0:256, 0:HD] = k[DEC:C0]
            kv[0:256, HD:2 * HD] = v[DEC:C0]
        if 5 <= i < 9:
            attend(q0, DEC, att0, i - 5, 256)
        accumulate(x1, acc1, ss1, slot)

    finish(acc1, ss1, kvs1, q1, C0, C1)
    kv_join[1].start()
    cache_swap.start()

    class Scatter:
        def __init__(self, bufs, att, rows, c):
            (self.s1, self.ra, self.rb, self.s2p, self.s2m, self.rm, self.rp,
             self.s3, self.fa, self.fb, self.gm, self.gp) = bufs
            self.att, self.c = att, c
            if rows == DEC:
                self.up = (slice(None), pl.ds(0, FS // 2))
                self.lo = (slice(None), pl.ds(FS // 2, FS // 2))
            else:
                self.up = (pl.ds(0, rows // 2), slice(None))
                self.lo = (pl.ds(rows // 2, rows // 2), slice(None))

        def term(self, kf, ks):
            slot = tp_of((f + offset_of(kf)) % 4, (s + offset_of(ks)) % 4)
            return mm(self.att[...], wo[:, pl.ds(pl.multiple_of(slot * FS, FS), FS)])

        def copy(self, src, dst, index, peer):
            return to_tp(src, dst, rs_send.at[self.c, index], rs_recv.at[self.c, index], peer)

        def merge(self, p, part, upper):
            axis = 1 if p.shape[0] == DEC else 0
            n = p.shape[axis] // 2
            a, b = lax.slice_in_dim(p, 0, n, axis=axis), lax.slice_in_dim(p, n, 2 * n, axis=axis)
            if upper:
                a = a + part.astype(F32)
            else:
                b = b + part.astype(F32)
            return jnp.concatenate([a, b], axis=axis).astype(BF16)

        def upper(self, k):
            return self.copy(self.s1.at[(k, *self.up)], self.ra.at[k], 4 * k, sn)

        def lower(self, k):
            return self.copy(self.s1.at[(k, *self.lo)], self.rb.at[k], 4 * k + 1, sp)

        def ahead(self, k):
            return self.copy(self.s2p.at[k], self.rm.at[k], 4 * k + 2, sn)

        def back(self, k):
            return self.copy(self.s2m.at[k], self.rp.at[k], 4 * k + 3, sp)

        def last(self):
            return [
                self.copy(self.s3.at[(0, *self.up)], self.fa, 16, fn),
                self.copy(self.s3.at[(0, *self.lo)], self.fb, 17, fp),
                self.copy(self.s3.at[1], self.gm, 18, fn),
                self.copy(self.s3.at[2], self.gp, 19, fp),
            ]

        def first_hop(self):
            @pl.loop(0, 4)
            def _(j):
                k = 3 - j
                self.s1[k] = self.term(k, 3).astype(BF16)
                self.upper(k).start()
                self.lower(k).start()

        def second_hop(self):
            @pl.loop(0, 4)
            def _(j):
                k = 3 - j
                p = self.term(k, 1)
                self.upper(k).wait_recv()
                self.s2p[k] = self.merge(p, self.ra[k], True)
                self.ahead(k).start()
                p = self.term(k, 2)
                self.lower(k).wait_recv()
                self.s2m[k] = self.merge(p, self.rb[k], False)
                self.back(k).start()

        def gathered(self, k):
            p = self.term(k, 0)
            self.ahead(k).wait_recv()
            self.back(k).wait_recv()
            return p + self.rm[k].astype(F32) + self.rp[k].astype(F32)

        def third_hop(self):
            c1, c2, c3, c4 = self.last()
            self.s3[0] = self.gathered(3).astype(BF16)
            c1.start()
            c2.start()
            p = self.gathered(1)
            c1.wait_recv()
            self.s3[1] = self.merge(p, self.fa[...], True)
            c3.start()
            p = self.gathered(2)
            c2.wait_recv()
            self.s3[2] = self.merge(p, self.fb[...], False)
            c4.start()

        def result(self):
            _, _, c3, c4 = self.last()
            p = self.gathered(0)
            c3.wait_recv()
            c4.wait_recv()
            return p + self.gm[...].astype(F32) + self.gp[...].astype(F32)

        def drain(self):
            for k in range(4):
                for c in (self.upper(k), self.lower(k), self.ahead(k), self.back(k)):
                    c.wait_send()
            for c in self.last():
                c.wait_send()

    sc0, sc1, scd = Scatter(rs0, att0, 256, 0), Scatter(rs1, att1, 256, 1), Scatter(rsd, attd, DEC, 2)

    loads[2].wait()
    sc0.first_hop()
    finish_q(acc1, ss1, q1, C0, C1)
    kv_join[1].wait_recv()
    k1, v1 = join(kvs1, kvr1, C0, C1)
    kv[256:512, 0:HD] = k1
    kv[256:512, HD:2 * HD] = v1
    sc0.second_hop()

    for h in range(4):
        attend(q1, 0, att1, h, 512)

    def group_copies(j):
        there = (g + j) % 8
        dev = (there, t)
        return (
            pltpu.make_async_remote_copy(pack.at[j], pool.at[j], grp_send.at[0, j], grp_recv.at[0, j],
                                         device_id=dev, device_id_type=MESH),
            pltpu.make_async_remote_copy(cnt_s.at[there], cnt_r.at[j], grp_send.at[1, j], grp_recv.at[1, j],
                                         device_id=dev, device_id_type=MESH),
        )

    @pl.loop(0, 8)
    def _(j):
        there = (g + j) % 8
        want = lax.broadcasted_iota(jnp.int32, (128, 512), 0) + there * 128
        hot = jnp.where(tok_slot[0:1, :] == want, 1.0, 0.0).astype(BF16)
        pages = mm(hot, kv[...]).astype(BF16)

        @pl.when(j == 0)
        def _():
            pool[0] = pages
            cnt_r[0] = cnt_s[there]

        @pl.when(j > 0)
        def _():
            pack[j] = pages
            for c in group_copies(j):
                c.start()

    sc1.first_hop()
    sc0.third_hop()
    sc1.second_hop()
    pre_out[0:256] = (sc0.result() + pre_in[0:256].astype(F32)).astype(BF16)

    loads[3].wait()
    cache_swap.wait_recv()
    q_swap.wait_recv()

    @pl.loop(1, 8)
    def _(j):
        for c in group_copies(j):
            c.wait_recv()

    mine = pl.ds(pl.multiple_of(half * 16, 16), 16)
    theirs = pl.ds(pl.multiple_of((1 - half) * 16, 16), 16)
    qa = jnp.concatenate(
        [q0[mine, h * HD:(h + 1) * HD] for h in range(4)] + [qx[:, h * HD:(h + 1) * HD] for h in range(4)],
        axis=0,
    )

    def halves(r, which):
        a, b = cache_own[r, which], cache_other[r, which]
        return jnp.where(half == 0, jnp.concatenate([a, b], axis=0), jnp.concatenate([b, a], axis=0))

    lane = lax.broadcasted_iota(jnp.int32, (HD, CACHE), 1)
    query = lax.broadcasted_iota(jnp.int32, (HD, CACHE), 0)
    scores = []
    for r in range(8):
        sc = mm(qa, halves(r, 0)) * scale
        ok = (query % 8 == r) & (lane < lens[half * 8 + r])
        scores.append(jnp.where(ok, sc, NEG_FILL))
    weight = []
    for src in range(8):
        sc = nt(qa, pool[src, :, 0:HD]) * scale
        slot = lax.broadcasted_iota(jnp.int32, (8, HD), 1) // 16
        at = pl.multiple_of((g + 8 - src) % 8 * HD, HD)
        m8 = jnp.where(slot.astype(F32) < cnt_r[src], mult[:, pl.ds(at, HD)], 0.0)
        m = jnp.concatenate([m8] * 16, axis=0)
        weight.append(m)
        scores.append(jnp.where(m > 0.0, sc, NEG_FILL))
    new = kvd[mine, :]
    new = jnp.concatenate([new, jnp.zeros((HD - 16, 2 * HD), BF16)], axis=0)
    col = lax.broadcasted_iota(jnp.int32, (HD, HD), 1)
    que = lax.broadcasted_iota(jnp.int32, (HD, HD), 0)
    ok = (col % 8 == que % 8) & (col // 8 <= que // 8 % 2)
    scores.append(jnp.where(ok, nt(qa, new[:, 0:HD]) * scale, NEG_FILL))
    top = scores[0].max(axis=1, keepdims=True)
    for sc in scores[1:]:
        top = jnp.maximum(top, sc.max(axis=1, keepdims=True))
    total = jnp.zeros((HD, 1), F32)
    mixed = jnp.zeros((HD, HD), F32)
    for i in range(17):
        e = jnp.exp(scores[i] - top)
        if 8 <= i < 16:
            e = e * weight[i - 8]
        total = total + jnp.sum(e, axis=1, keepdims=True)
        e = e.astype(BF16)
        if i < 8:
            mixed = mixed + nt(e, halves(i, 1))
        elif i < 16:
            mixed = mixed + mm(e, pool[i - 8, :, HD:2 * HD])
        else:
            mixed = mixed + mm(e, new[:, HD:2 * HD])
    mixed = (mixed / total).astype(BF16)
    for h in range(4):
        attd[mine, h * HD:(h + 1) * HD] = mixed[h * 16:(h + 1) * 16]
        ox_s[:, h * HD:(h + 1) * HD] = mixed[64 + h * 16:64 + (h + 1) * 16]
    o_swap.start()
    sc1.third_hop()
    o_swap.wait_recv()
    attd[theirs, :] = ox_r[...]
    scd.first_hop()
    scd.second_hop()
    pre_out[256:512] = (sc1.result() + pre_in[256:512].astype(F32)).astype(BF16)
    scd.third_hop()
    dsum = scd.result()
    dsum = jnp.concatenate([dsum[0:8], dsum[16:24], dsum[8:16], dsum[24:32]], axis=0)
    dec_out[...] = (dsum + dec_in[...].astype(F32)).astype(BF16)

    ag0.drain()
    ag1.drain()
    sc0.drain()
    sc1.drain()
    scd.drain()
    for c in kv_join + [q_swap, cache_swap, o_swap]:
        c.wait_send()

    @pl.loop(1, 8)
    def _(j):
        for c in group_copies(j):
            c.wait_send()


def scatter_bufs(rows):
    h, w = (rows, FS // 2) if rows == DEC else (rows // 2, FS)
    return (
        pltpu.VMEM((4, rows, FS), BF16),
        pltpu.VMEM((4, h, w), BF16),
        pltpu.VMEM((4, h, w), BF16),
        pltpu.VMEM((4, rows, FS), BF16),
        pltpu.VMEM((4, rows, FS), BF16),
        pltpu.VMEM((4, rows, FS), BF16),
        pltpu.VMEM((4, rows, FS), BF16),
        pltpu.VMEM((3, rows, FS), BF16),
        pltpu.VMEM((h, w), BF16),
        pltpu.VMEM((h, w), BF16),
        pltpu.VMEM((rows, FS), BF16),
        pltpu.VMEM((rows, FS), BF16),
    )


def body(
    prefill_in, decode_in, norm_gain, query_weight, query_bias, keyval_weight, keyval_bias,
    out_weight, pass_offset, routing, cache_len, page_table, cache_keyval,
):
    half_lanes = np.arange(HD) % 64
    freq = jnp.asarray((1000000.0 ** (-(half_lanes * (2.0 / HD)))).astype(np.float32).reshape(1, HD))
    vmem = pl.BlockSpec(memory_space=pltpu.VMEM)
    smem = pl.BlockSpec(memory_space=pltpu.SMEM)
    hbm = pl.BlockSpec(memory_space=pl.ANY)
    pre, dec = pl.pallas_call(
        kernel,
        out_shape=(
            jax.ShapeDtypeStruct((512, FS), BF16),
            jax.ShapeDtypeStruct((DEC, FS), BF16),
        ),
        in_specs=[vmem] * 6 + [smem] * 4 + [hbm] * 4,
        out_specs=(vmem, vmem),
        scratch_shapes=[
            pltpu.VMEM((16, 2, C0 // 2, FS), BF16),
            pltpu.VMEM((16, 2, C1 // 2, FS), BF16),
            pltpu.VMEM((WIDTH, FS), BF16),
            pltpu.VMEM((HD, WIDTH), BF16),
            pltpu.VMEM((FS, WIDTH), BF16),
            pltpu.VMEM((C0, 640), F32),
            pltpu.VMEM((C1, 640), F32),
            pltpu.VMEM((C0, HD), F32),
            pltpu.VMEM((C1, HD), F32),
            pltpu.VMEM((C0 + C1, HD), F32),
            pltpu.VMEM((C0 + C1, HD), F32),
            pltpu.VMEM((C0, FS), BF16),
            pltpu.VMEM((C1, FS), BF16),
            pltpu.VMEM((C0, HD), BF16),
            pltpu.VMEM((C1, HD), BF16),
            pltpu.VMEM((C0, HD), BF16),
            pltpu.VMEM((C1, HD), BF16),
            pltpu.VMEM((512, 2 * HD), BF16),
            pltpu.VMEM((DEC, 2 * HD), BF16),
            pltpu.VMEM((256, FS), BF16),
            pltpu.VMEM((256, FS), BF16),
            pltpu.VMEM((DEC, FS), BF16),
            pltpu.VMEM((8, 2, 64, CACHE), BF16),
            pltpu.VMEM((8, 2, 64, CACHE), BF16),
            pltpu.VMEM((8, HD, 2 * HD), BF16),
            pltpu.VMEM((8, HD, 2 * HD), BF16),
            pltpu.VMEM((8, 8, HD), F32),
            pltpu.VMEM((8, 8, HD), F32),
            pltpu.VMEM((16, FS), BF16),
            pltpu.VMEM((16, FS), BF16),
            pltpu.VMEM((16, FS), BF16),
            pltpu.VMEM((8, 1024), F32),
            pltpu.VMEM((8, 512), jnp.int32),
            scatter_bufs(256),
            scatter_bufs(256),
            scatter_bufs(DEC),
            pltpu.SemaphoreType.DMA((4,)),
            pltpu.SemaphoreType.DMA((2, 20)),
            pltpu.SemaphoreType.DMA((2, 20)),
            pltpu.SemaphoreType.DMA((3, 20)),
            pltpu.SemaphoreType.DMA((3, 20)),
            pltpu.SemaphoreType.DMA((5,)),
            pltpu.SemaphoreType.DMA((5,)),
            pltpu.SemaphoreType.DMA((2, 8)),
            pltpu.SemaphoreType.DMA((2, 8)),
        ],
        compiler_params=pltpu.CompilerParams(
            collective_id=0, has_side_effects=True, vmem_limit_bytes=62 * 2**20
        ),
    )(
        prefill_in,
        decode_in.reshape(DEC, FS),
        norm_gain.reshape(1, WIDTH),
        query_bias.reshape(1, FS),
        keyval_bias.reshape(1, HD),
        freq,
        pass_offset,
        routing.reshape(32),
        cache_len,
        page_table.T,
        query_weight,
        keyval_weight.transpose(1, 2, 0).reshape(HD, WIDTH),
        out_weight,
        cache_keyval.transpose(0, 2, 3, 1),
    )
    return pre, dec.reshape(2, 16, FS)


def solution(mesh):
    in_specs = (
        P("group", "tp"),
        P(None, "group", "tp"),
        P(),
        P(None, "tp"),
        P("tp"),
        P(None, None, "tp"),
        P(None, "tp"),
        P("tp", None),
        P("group"),
        P("group", None),
        P("group"),
        P("group", None),
        P("group", None, None, "tp"),
    )
    out_specs = (P("group", "tp"), P(None, "group", "tp"))
    return jax.shard_map(body, mesh=mesh, in_specs=in_specs, out_specs=out_specs, check_vma=False)
```

```python
import jax
import jax.numpy as jnp
import numpy as np
from jax import lax
from jax.experimental import pallas as pl
from jax.experimental.pallas import tpu as pltpu
from jax.sharding import PartitionSpec as P

MESH = pl.DeviceIdType.MESH
F32 = jnp.float32
BF16 = jnp.bfloat16
HD = 128
FS = 512
C0, C1 = 288, 256
DEC = 32
NEG_FILL = -1e30
EPSILON = 1e-06
CACHE = 256
WIDTH = 8192


def nt(a, b):
    return lax.dot_general(a, b, (((1,), (1,)), ((), ())), preferred_element_type=F32)


def mm(a, b):
    return jnp.dot(a, b, preferred_element_type=F32)


def offset_of(k):
    return k + k // 2 - 2 * (k // 3)


def kernel(
    pre_in, dec_in, gain, qbias, kvbias, freq, offset, routing, lens, table,
    wq_hbm, wkv_hbm, wo_hbm, cache_hbm,
    pre_out, dec_out,
    params, x0, x1, wq, wkv, wo, acc0, acc1, ss0, ss1, cos_t, sin_t,
    q0, q1, kvs0, kvs1, kvr0, kvr1, kv, kvd, att0, att1, attd,
    cache, s8, sx, e_own, ex, o8, ox, m_c, l_c, pack, pool, cnt_s, cnt_r, qx, mult,
    tok_slot,
    rs0, rs1, rsd,
    w_sem, ag_send, ag_recv, rs_send, rs_recv, pair_send, pair_recv, grp_send, grp_recv,
):
    g = lax.axis_index("group")
    t = lax.axis_index("tp")
    core = g % 2
    y, z = t // 4, t % 4
    f = z + core * (y - z)
    s = y + core * (z - y)

    def tp_of(ff, ss):
        return 4 * ss + ff + core * 3 * (ff - ss)

    fn, fp = tp_of((f + 1) % 4, s), tp_of((f + 3) % 4, s)
    sn, sp = tp_of(f, (s + 1) % 4), tp_of(f, (s + 3) % 4)
    pair = t + 1 - 2 * (t % 2)
    half = t % 2

    drows = dec_in[...].astype(F32)
    drows = jnp.concatenate([drows[0:8], drows[16:24], drows[8:16], drows[24:32]], axis=0)
    first = jnp.concatenate([drows.astype(BF16), pre_in[0:256]], axis=0)
    x0[0] = first.reshape(2, C0 // 2, FS)
    x1[0] = pre_in[256:512].reshape(2, C1 // 2, FS)

    barrier = pltpu.get_barrier_semaphore()
    for peer in (fn, fp, sn, sp):
        pl.semaphore_signal(barrier, inc=1, device_id=(g, peer), device_id_type=MESH)
    for j in range(1, 8):
        pl.semaphore_signal(barrier, inc=1, device_id=((g + j) % 8, t), device_id_type=MESH)

    loads = [
        pltpu.make_async_copy(wq_hbm, wq, w_sem.at[0]),
        pltpu.make_async_copy(wkv_hbm, wkv, w_sem.at[1]),
        pltpu.make_async_copy(wo_hbm, wo, w_sem.at[2]),
        pltpu.make_async_copy(cache_hbm, cache, w_sem.at[3]),
    ]
    for load in loads:
        load.start()

    pl.semaphore_wait(barrier, 11)

    def to_tp(src, dst, send, recv, peer):
        return pltpu.make_async_remote_copy(src, dst, send, recv, device_id=(g, peer), device_id_type=MESH)

    class Gather:
        def __init__(self, x, rows, c):
            self.x, self.c, self.sent = x, c, []

        def copy(self, src, dst, part, index, peer):
            src, dst = 4 * src[0] + src[1], 4 * dst[0] + dst[1]
            src = self.x.at[src] if part is None else self.x.at[src, part]
            dst = self.x.at[dst] if part is None else self.x.at[dst, part]
            return to_tp(src, dst, ag_send.at[self.c, index], ag_recv.at[self.c, index], peer)

        def go(self, src, dst, part, index, peer):
            copy = self.copy(src, dst, part, index, peer)
            copy.start()
            self.sent.append(copy)

        def came(self, dst, part, index):
            self.copy(dst, dst, part, index, fn).wait_recv()

        def send_own(self):
            self.go((0, 0), (2, 0), None, 0, fn)
            self.go((0, 0), (1, 0), None, 1, fp)
            self.line(0)

        def line(self, k):
            self.go((k, 0), (k, 2), None, 4 + 4 * k, sn)
            self.go((k, 0), (k, 1), None, 5 + 4 * k, sp)

        def near(self):
            self.came((2, 0), None, 0)
            self.go((2, 0), (3, 0), 0, 2, fn)
            self.line(2)
            self.came((1, 0), None, 1)
            self.go((1, 0), (3, 0), 1, 3, fp)
            self.line(1)

        def far(self):
            self.came((3, 0), 0, 2)
            self.came((3, 0), 1, 3)
            self.line(3)

        def step(self, i):
            j, w = (i - 3) // 3, (i - 3) % 3
            if i < 3:
                if i == 1:
                    self.near()
                return i, 0
            if i == 5:
                self.far()
                return 3, 0
            if i == 15 or w == 2:
                self.came((j - 1, 3), 0, 2 + 4 * j)
                self.came((j - 1, 3), 1, 3 + 4 * j)
                return j - 1, 3
            if w == 0:
                self.came((j, 2), None, 4 + 4 * j)
                self.go((j, 2), (j, 3), 0, 6 + 4 * j, sn)
                return j, 2
            self.came((j, 1), None, 5 + 4 * j)
            self.go((j, 1), (j, 3), 1, 7 + 4 * j, sp)
            return j, 1

        def drain(self):
            for copy in self.sent:
                copy.wait_send()

    ag0, ag1 = Gather(x0, C0, 0), Gather(x1, C1, 1)
    ag0.send_own()
    ag1.send_own()

    def accumulate(x, acc, ss, place):
        kf, ks = place
        slot = tp_of((f + offset_of(kf)) % 4, (s + offset_of(ks)) % 4)
        at = pl.multiple_of(slot * FS, FS)
        xf = x[4 * kf + ks].reshape(-1, FS).astype(F32)
        sq = xf * xf
        ss[...] += sq[:, 0:128] + sq[:, 128:256] + sq[:, 256:384] + sq[:, 384:512]
        xg = (xf * params[pl.ds(slot, 1), :]).astype(BF16)
        acc[:, 0:512] += mm(xg, wq[pl.ds(at, FS), :])
        acc[:, 512:640] += nt(xg, wkv[:, pl.ds(at, FS)])

    for i in range(16):
        params[i:i + 1] = gain[i * FS:(i + 1) * FS].astype(F32).reshape(1, FS)
    params[16:17] = qbias[...].astype(F32).reshape(1, FS)
    params[17:18, 0:HD] = jnp.concatenate([kvbias[0:1].astype(F32), kvbias[1:2].astype(F32)], axis=1)
    acc0[...] = jnp.zeros_like(acc0)
    acc1[...] = jnp.zeros_like(acc1)
    ss0[...] = jnp.zeros_like(ss0)
    ss1[...] = jnp.zeros_like(ss1)
    loads[0].wait()
    loads[1].wait()

    gathers = ((ag0, x0, acc0, ss0), (ag1, x1, acc1, ss1))

    def advance(c, *steps):
        ag, x, acc, ss = gathers[c]
        for place in [ag.step(i) for i in steps]:
            accumulate(x, acc, ss, place)

    advance(0, 0, 1, 2, 3, 4)
    advance(0, 5)

    advance(1, 0, 1, 2, 3, 4)
    advance(0, 6, 7, 8)
    advance(1, 5)
    advance(0, 9, 10, 11)
    advance(1, 6, 7, 8)
    advance(0, 12, 13)

    lane = lax.broadcasted_iota(jnp.int32, (C0, HD), 1)
    row = lax.broadcasted_iota(jnp.int32, (C0, HD), 0)
    places = row - DEC + offset[0]
    for r in range(16):
        base = (r // 8) * 16 + r % 8
        places = jnp.where(row == base, lens[r], places)
        places = jnp.where(row == base + 8, lens[r] + 1, places)
    sign = jnp.where(lane < 64, -1.0, 1.0).astype(F32)
    angle = places.astype(F32) * freq[...]
    cos_t[0:C0] = jnp.cos(angle)
    sin_t[0:C0] = jnp.sin(angle) * sign
    angle = (row[0:C1] + (C1 + offset[0])).astype(F32) * freq[...]
    cos_t[C0:C0 + C1] = jnp.cos(angle)
    sin_t[C0:C0 + C1] = jnp.sin(angle) * sign[0:C1]

    token = lax.broadcasted_iota(jnp.int32, (8, 512), 1)

    def rank_block(b, carry):
        slots, counts = carry
        d = routing[b]
        rank = jnp.int32(0)
        for k in range(8):
            rank = rank + jnp.where(d == k, counts[k], 0)
        slots = jnp.where(token // 16 == b, d * 128 + rank * 16 + token % 16, slots)
        return slots, tuple(counts[k] + jnp.where(d == k, 1, 0) for k in range(8))

    slots, counts = lax.fori_loop(
        0, 32, rank_block, (jnp.zeros((8, 512), jnp.int32), (jnp.int32(0),) * 8)
    )
    tok_slot[...] = slots
    for k in range(8):
        cnt_s[k] = jnp.full((8, 128), 1.0, F32) * counts[k].astype(F32)

    page = lax.broadcasted_iota(jnp.int32, (16, 1024), 1) // 16
    prow = lax.broadcasted_iota(jnp.int32, (16, 1024), 0)

    def count_pages(i, times):
        r, j = i // 8, i % 8
        return times + jnp.where((prow == r) & (page == table[j, r]), 1.0, 0.0)

    mult[...] = lax.fori_loop(0, 128, count_pages, jnp.zeros((16, 1024), F32))

    advance(0, 14, 15)

    def finish(acc, ss, kvs, q, table_at, rows):
        inv = lax.rsqrt(jnp.sum(ss[...], axis=1, keepdims=True) * (1.0 / WIDTH) + EPSILON)
        kvs[...] = (acc[:, 512:640] * inv + params[17:18, 0:HD]).astype(BF16)
        return inv

    def finish_q(acc, ss, q, table_at, rows):
        inv = lax.rsqrt(jnp.sum(ss[...], axis=1, keepdims=True) * (1.0 / WIDTH) + EPSILON)
        c, sn_ = cos_t[table_at:table_at + rows], sin_t[table_at:table_at + rows]
        for h in range(4):
            at = slice(h * HD, (h + 1) * HD)
            v = acc[:, at] * inv + params[16:17, at]
            q[:, at] = (v * c + pltpu.roll(v, 64, 1) * sn_).astype(BF16)

    def join(own, other, table_at, rows):
        a, b = own[...].astype(F32), other[...].astype(F32)
        lo = jnp.where(half == 0, a, b)
        hi = jnp.where(half == 0, b, a)
        low = lax.broadcasted_iota(jnp.int32, (rows, HD), 1) < 64
        k = jnp.where(low, lo, pltpu.roll(hi, 64, 1))
        v = jnp.where(low, pltpu.roll(lo, 64, 1), hi)
        k = k * cos_t[table_at:table_at + rows] + pltpu.roll(k, 64, 1) * sin_t[table_at:table_at + rows]
        return k.astype(BF16), v.astype(BF16)

    def pair_copy(src, dst, index):
        return to_tp(src, dst, pair_send.at[index], pair_recv.at[index], pair)

    kv_join = [pair_copy(kvs0, kvr0, 0), pair_copy(kvs1, kvr1, 1)]
    q_swap = pair_copy(q0.at[pl.ds(0, DEC)], qx, 2)
    s_swap = pair_copy(s8.at[pl.ds(HD, HD)], sx, 3)
    e_swap = pair_copy(e_own, ex, 4)
    o_swap = pair_copy(o8.at[pl.ds(HD, HD)], ox, 5)

    scale = HD ** (-0.5)

    def attend(q, start, att, h, keys):
        at = pl.ds(h * HD, HD)
        sc = nt(q[start:start + 256, at], kv[0:keys, 0:HD]) * scale
        qi = lax.broadcasted_iota(jnp.int32, (256, keys), 0) + (keys - 256)
        ki = lax.broadcasted_iota(jnp.int32, (256, keys), 1)
        sc = jnp.where(ki <= qi, sc, NEG_FILL)
        e = jnp.exp(sc - jnp.max(sc, axis=1, keepdims=True))
        total = jnp.sum(e, axis=1, keepdims=True)
        att[:, at] = (mm(e.astype(BF16), kv[0:keys, HD:2 * HD]) / total).astype(BF16)

    def query_row(shape):
        m = lax.broadcasted_iota(jnp.int32, shape, 0)
        return m % DEC // 16 * 8 + m % 8

    def by_head(ref):
        return jnp.concatenate([ref[0:DEC, h * HD:(h + 1) * HD] for h in range(4)], axis=0)

    def padded(part):
        zero = jnp.zeros((64, CACHE), BF16)
        return jnp.where(half == 0, jnp.concatenate([part, zero], axis=0), jnp.concatenate([zero, part], axis=0))

    def cache_scores():
        q_swap.wait_recv()
        loads[3].wait()
        q8 = jnp.concatenate([by_head(q0), by_head(qx)], axis=0)
        s8[...] = jnp.zeros_like(s8)

        @pl.loop(0, 16)
        def _(r):
            s8[...] = jnp.where(query_row((256, CACHE)) == r, mm(q8, padded(cache[r, 0])), s8[...])

        s_swap.start()

    def cache_weights():
        s_swap.wait_recv()
        owner = query_row((HD, CACHE))
        length = jnp.zeros((HD, CACHE), jnp.int32)
        for r in range(16):
            length = jnp.where(owner == r, lens[r], length)
        sc = (s8[0:HD] + sx[...]) * scale
        sc = jnp.where(lax.broadcasted_iota(jnp.int32, (HD, CACHE), 1) < length, sc, NEG_FILL)
        top = jnp.max(sc, axis=1, keepdims=True)
        e = jnp.exp(sc - top)
        m_c[...] = jnp.broadcast_to(top, (HD, HD))
        l_c[...] = jnp.broadcast_to(jnp.sum(e, axis=1, keepdims=True), (HD, HD))
        e_own[...] = e.astype(BF16)
        e_swap.start()

    def cache_values():
        e_swap.wait_recv()
        e8 = jnp.concatenate([e_own[...], ex[...]], axis=0)
        o8[...] = jnp.zeros_like(o8)

        @pl.loop(0, 16)
        def _(r):
            o8[...] = jnp.where(query_row((256, HD)) == r, nt(e8, padded(cache[r, 1])), o8[...])

        o_swap.start()

    def pass_keys(c, kvs, kvr, at, rows):
        kv_join[c].wait_recv()
        k, v = join(kvs, kvr, at, rows)
        if c == 0:
            kvd[:, 0:HD] = k[0:DEC]
            kvd[:, HD:2 * HD] = v[0:DEC]
            k, v = k[DEC:C0], v[DEC:C0]
        kv[256 * c:256 * (c + 1), 0:HD] = k
        kv[256 * c:256 * (c + 1), HD:2 * HD] = v

    class Scatter:
        def __init__(self, bufs, att, rows, c):
            (self.s1, self.ra, self.rb, self.s2p, self.s2m, self.rm, self.rp,
             self.s3, self.fa, self.fb, self.gm, self.gp) = bufs
            self.att, self.c = att, c
            if rows == DEC:
                self.up = (slice(None), pl.ds(0, FS // 2))
                self.lo = (slice(None), pl.ds(FS // 2, FS // 2))
            else:
                self.up = (pl.ds(0, rows // 2), slice(None))
                self.lo = (pl.ds(rows // 2, rows // 2), slice(None))

        def term(self, kf, ks):
            slot = tp_of((f + offset_of(kf)) % 4, (s + offset_of(ks)) % 4)
            return mm(self.att[...], wo[:, pl.ds(pl.multiple_of(slot * FS, FS), FS)])

        def copy(self, src, dst, index, peer):
            return to_tp(src, dst, rs_send.at[self.c, index], rs_recv.at[self.c, index], peer)

        def merge(self, p, part, upper):
            axis = 1 if p.shape[0] == DEC else 0
            n = p.shape[axis] // 2
            a, b = lax.slice_in_dim(p, 0, n, axis=axis), lax.slice_in_dim(p, n, 2 * n, axis=axis)
            if upper:
                a = a + part.astype(F32)
            else:
                b = b + part.astype(F32)
            return jnp.concatenate([a, b], axis=axis).astype(BF16)

        def upper(self, k):
            return self.copy(self.s1.at[(k, *self.up)], self.ra.at[k], 4 * k, sn)

        def lower(self, k):
            return self.copy(self.s1.at[(k, *self.lo)], self.rb.at[k], 4 * k + 1, sp)

        def ahead(self, k):
            return self.copy(self.s2p.at[k], self.rm.at[k], 4 * k + 2, sn)

        def back(self, k):
            return self.copy(self.s2m.at[k], self.rp.at[k], 4 * k + 3, sp)

        def last(self):
            return [
                self.copy(self.s3.at[(0, *self.up)], self.fa, 16, fn),
                self.copy(self.s3.at[(0, *self.lo)], self.fb, 17, fp),
                self.copy(self.s3.at[1], self.gm, 18, fn),
                self.copy(self.s3.at[2], self.gp, 19, fp),
            ]

        def first_hop(self):
            @pl.loop(0, 4)
            def _(j):
                k = 3 - j
                self.s1[k] = self.term(k, 3).astype(BF16)
                self.upper(k).start()
                self.lower(k).start()

        def second_hop(self):
            @pl.loop(0, 4)
            def _(j):
                k = 3 - j
                p = self.term(k, 1)
                self.upper(k).wait_recv()
                self.s2p[k] = self.merge(p, self.ra[k], True)
                self.ahead(k).start()
                p = self.term(k, 2)
                self.lower(k).wait_recv()
                self.s2m[k] = self.merge(p, self.rb[k], False)
                self.back(k).start()

        def gathered(self, k):
            p = self.term(k, 0)
            self.ahead(k).wait_recv()
            self.back(k).wait_recv()
            return p + self.rm[k].astype(F32) + self.rp[k].astype(F32)

        def third_hop(self):
            c1, c2, c3, c4 = self.last()
            self.s3[0] = self.gathered(3).astype(BF16)
            c1.start()
            c2.start()
            p = self.gathered(1)
            c1.wait_recv()
            self.s3[1] = self.merge(p, self.fa[...], True)
            c3.start()
            p = self.gathered(2)
            c2.wait_recv()
            self.s3[2] = self.merge(p, self.fb[...], False)
            c4.start()

        def result(self):
            _, _, c3, c4 = self.last()
            p = self.gathered(0)
            c3.wait_recv()
            c4.wait_recv()
            return p + self.gm[...].astype(F32) + self.gp[...].astype(F32)

        def drain(self):
            for k in range(4):
                for c in (self.upper(k), self.lower(k), self.ahead(k), self.back(k)):
                    c.wait_send()
            for c in self.last():
                c.wait_send()

    sc0, sc1, scd = Scatter(rs0, att0, 256, 0), Scatter(rs1, att1, 256, 1), Scatter(rsd, attd, DEC, 2)

    def group_copies(j):
        there = (g + j) % 8
        dev = (there, t)
        return (
            pltpu.make_async_remote_copy(pack.at[j], pool.at[j], grp_send.at[0, j], grp_recv.at[0, j],
                                         device_id=dev, device_id_type=MESH),
            pltpu.make_async_remote_copy(cnt_s.at[there], cnt_r.at[j], grp_send.at[1, j], grp_recv.at[1, j],
                                         device_id=dev, device_id_type=MESH),
        )

    def send_pages():
        @pl.loop(0, 8)
        def _(j):
            there = (g + j) % 8
            want = lax.broadcasted_iota(jnp.int32, (128, 512), 0) + there * 128
            hot = jnp.where(tok_slot[0:1, :] == want, 1.0, 0.0).astype(BF16)
            pages = mm(hot, kv[...]).astype(BF16)

            @pl.when(j == 0)
            def _():
                pool[0] = pages
                cnt_r[0] = cnt_s[there]

            @pl.when(j > 0)
            def _():
                pack[j] = pages
                for c in group_copies(j):
                    c.start()

    def decode_rows():
        @pl.loop(1, 8)
        def _(j):
            for c in group_copies(j):
                c.wait_recv()

        qa = by_head(q0)
        scores, weight = [], []
        for src in range(8):
            sc = nt(qa, pool[src, :, 0:HD]) * scale
            slot = lax.broadcasted_iota(jnp.int32, (16, HD), 1) // 16
            at = pl.multiple_of((g + 8 - src) % 8 * HD, HD)
            m16 = jnp.where(slot.astype(F32) < cnt_r[src, 0:1], mult[:, pl.ds(at, HD)], 0.0)
            m = jnp.concatenate([m16[0:8], m16[0:8], m16[8:16], m16[8:16]] * 4, axis=0)
            weight.append(m)
            scores.append(jnp.where(m > 0.0, sc, NEG_FILL))
        new = jnp.concatenate([kvd[...], jnp.zeros((HD - DEC, 2 * HD), BF16)], axis=0)
        col = lax.broadcasted_iota(jnp.int32, (HD, HD), 1)
        same = (col // 16 * 8 + col % 8 == query_row((HD, HD))) & (col < DEC)
        step = lax.broadcasted_iota(jnp.int32, (HD, HD), 0) // 8 % 2
        ok = same & (col // 8 % 2 <= step)
        scores.append(jnp.where(ok, nt(qa, new[:, 0:HD]) * scale, NEG_FILL))
        top = m_c[...]
        for sc in scores:
            top = jnp.maximum(top, jnp.max(sc, axis=1, keepdims=True))
        o_swap.wait_recv()
        old = jnp.exp(m_c[...] - top)
        total = l_c[...] * old
        mixed = (o8[0:HD] + ox[...]) * old
        for i in range(9):
            e = jnp.exp(scores[i] - top)
            if i < 8:
                e = e * weight[i]
            total = total + jnp.sum(e, axis=1, keepdims=True)
            values = pool[i, :, HD:2 * HD] if i < 8 else new[:, HD:2 * HD]
            mixed = mixed + mm(e.astype(BF16), values)
        mixed = (mixed / total).astype(BF16)
        for h in range(4):
            attd[:, h * HD:(h + 1) * HD] = mixed[h * DEC:(h + 1) * DEC]

    finish(acc0, ss0, kvs0, q0, 0, C0)
    kv_join[0].start()
    finish_q(acc0, ss0, q0, 0, C0)
    q_swap.start()
    advance(1, 9, 10, 11)
    pass_keys(0, kvs0, kvr0, 0, C0)
    for h in range(4):
        attend(q0, DEC, att0, h, 256)
    loads[2].wait()
    sc0.first_hop()
    advance(1, 12, 13)
    cache_scores()
    advance(1, 14, 15)
    finish(acc1, ss1, kvs1, q1, C0, C1)
    kv_join[1].start()
    cache_weights()
    finish_q(acc1, ss1, q1, C0, C1)
    sc0.second_hop()
    pass_keys(1, kvs1, kvr1, C0, C1)
    send_pages()
    cache_values()
    for h in range(4):
        attend(q1, 0, att1, h, 512)
    sc1.first_hop()
    sc0.third_hop()
    decode_rows()
    scd.first_hop()
    sc1.second_hop()
    scd.second_hop()
    pre_out[0:256] = (sc0.result() + pre_in[0:256].astype(F32)).astype(BF16)
    sc1.third_hop()
    scd.third_hop()
    pre_out[256:512] = (sc1.result() + pre_in[256:512].astype(F32)).astype(BF16)
    dsum = scd.result()
    dsum = jnp.concatenate([dsum[0:8], dsum[16:24], dsum[8:16], dsum[24:32]], axis=0)
    dec_out[...] = (dsum + dec_in[...].astype(F32)).astype(BF16)

    ag0.drain()
    ag1.drain()
    sc0.drain()
    sc1.drain()
    scd.drain()
    for c in kv_join + [q_swap, s_swap, e_swap, o_swap]:
        c.wait_send()

    @pl.loop(1, 8)
    def _(j):
        for c in group_copies(j):
            c.wait_send()


def scatter_bufs(rows):
    h, w = (rows, FS // 2) if rows == DEC else (rows // 2, FS)
    return (
        pltpu.VMEM((4, rows, FS), BF16),
        pltpu.VMEM((4, h, w), BF16),
        pltpu.VMEM((4, h, w), BF16),
        pltpu.VMEM((4, rows, FS), BF16),
        pltpu.VMEM((4, rows, FS), BF16),
        pltpu.VMEM((4, rows, FS), BF16),
        pltpu.VMEM((4, rows, FS), BF16),
        pltpu.VMEM((3, rows, FS), BF16),
        pltpu.VMEM((h, w), BF16),
        pltpu.VMEM((h, w), BF16),
        pltpu.VMEM((rows, FS), BF16),
        pltpu.VMEM((rows, FS), BF16),
    )


def body(
    prefill_in, decode_in, norm_gain, query_weight, query_bias, keyval_weight, keyval_bias,
    out_weight, pass_offset, routing, cache_len, page_table, cache_keyval,
):
    half_lanes = np.arange(HD) % 64
    freq = jnp.asarray((1000000.0 ** (-(half_lanes * (2.0 / HD)))).astype(np.float32).reshape(1, HD))
    vmem = pl.BlockSpec(memory_space=pltpu.VMEM)
    smem = pl.BlockSpec(memory_space=pltpu.SMEM)
    hbm = pl.BlockSpec(memory_space=pl.ANY)
    pre, dec = pl.pallas_call(
        kernel,
        out_shape=(
            jax.ShapeDtypeStruct((512, FS), BF16),
            jax.ShapeDtypeStruct((DEC, FS), BF16),
        ),
        in_specs=[vmem] * 6 + [smem] * 4 + [hbm] * 4,
        out_specs=(vmem, vmem),
        scratch_shapes=[
            pltpu.VMEM((18, FS), F32),
            pltpu.VMEM((16, 2, C0 // 2, FS), BF16),
            pltpu.VMEM((16, 2, C1 // 2, FS), BF16),
            pltpu.VMEM((WIDTH, FS), BF16),
            pltpu.VMEM((HD, WIDTH), BF16),
            pltpu.VMEM((FS, WIDTH), BF16),
            pltpu.VMEM((C0, 640), F32),
            pltpu.VMEM((C1, 640), F32),
            pltpu.VMEM((C0, HD), F32),
            pltpu.VMEM((C1, HD), F32),
            pltpu.VMEM((C0 + C1, HD), F32),
            pltpu.VMEM((C0 + C1, HD), F32),
            pltpu.VMEM((C0, FS), BF16),
            pltpu.VMEM((C1, FS), BF16),
            pltpu.VMEM((C0, HD), BF16),
            pltpu.VMEM((C1, HD), BF16),
            pltpu.VMEM((C0, HD), BF16),
            pltpu.VMEM((C1, HD), BF16),
            pltpu.VMEM((512, 2 * HD), BF16),
            pltpu.VMEM((DEC, 2 * HD), BF16),
            pltpu.VMEM((256, FS), BF16),
            pltpu.VMEM((256, FS), BF16),
            pltpu.VMEM((DEC, FS), BF16),
            pltpu.VMEM((16, 2, 64, CACHE), BF16),
            pltpu.VMEM((256, CACHE), F32),
            pltpu.VMEM((HD, CACHE), F32),
            pltpu.VMEM((HD, CACHE), BF16),
            pltpu.VMEM((HD, CACHE), BF16),
            pltpu.VMEM((256, HD), F32),
            pltpu.VMEM((HD, HD), F32),
            pltpu.VMEM((HD, HD), F32),
            pltpu.VMEM((HD, HD), F32),
            pltpu.VMEM((8, HD, 2 * HD), BF16),
            pltpu.VMEM((8, HD, 2 * HD), BF16),
            pltpu.VMEM((8, 8, HD), F32),
            pltpu.VMEM((8, 8, HD), F32),
            pltpu.VMEM((DEC, FS), BF16),
            pltpu.VMEM((16, 1024), F32),
            pltpu.VMEM((8, 512), jnp.int32),
            scatter_bufs(256),
            scatter_bufs(256),
            scatter_bufs(DEC),
            pltpu.SemaphoreType.DMA((4,)),
            pltpu.SemaphoreType.DMA((2, 20)),
            pltpu.SemaphoreType.DMA((2, 20)),
            pltpu.SemaphoreType.DMA((3, 20)),
            pltpu.SemaphoreType.DMA((3, 20)),
            pltpu.SemaphoreType.DMA((6,)),
            pltpu.SemaphoreType.DMA((6,)),
            pltpu.SemaphoreType.DMA((2, 8)),
            pltpu.SemaphoreType.DMA((2, 8)),
        ],
        compiler_params=pltpu.CompilerParams(
            collective_id=0, has_side_effects=True, vmem_limit_bytes=62 * 2**20
        ),
    )(
        prefill_in,
        decode_in.reshape(DEC, FS),
        norm_gain,
        query_bias,
        keyval_bias,
        freq,
        pass_offset,
        routing.reshape(32),
        cache_len,
        page_table.T,
        query_weight,
        keyval_weight.transpose(1, 2, 0).reshape(HD, WIDTH),
        out_weight,
        cache_keyval.transpose(0, 2, 3, 1),
    )
    return pre, dec.reshape(2, 16, FS)


def solution(mesh):
    in_specs = (
        P("group", "tp"),
        P(None, "group", "tp"),
        P(),
        P(None, "tp"),
        P("tp"),
        P(None, None, "tp"),
        P(None, "tp"),
        P("tp", None),
        P("group"),
        P("group", None),
        P("group"),
        P("group", None),
        P("group", None, None, "tp"),
    )
    out_specs = (P("group", "tp"), P(None, "group", "tp"))
    return jax.shard_map(body, mesh=mesh, in_specs=in_specs, out_specs=out_specs, check_vma=False)
```

```python
import jax
import jax.numpy as jnp
import numpy as np
from jax import lax
from jax.experimental import pallas as pl
from jax.experimental.pallas import tpu as pltpu
from jax.sharding import PartitionSpec as P

MESH = pl.DeviceIdType.MESH
F32 = jnp.float32
BF16 = jnp.bfloat16
HD = 128
FS = 512
DEC = 32
T0, T1 = 256, 256
C0, C1 = DEC + T0, T1
NEG_FILL = -1e30
EPSILON = 1e-06
CACHE = 256
WIDTH = 8192


def nt(a, b):
    return lax.dot_general(a, b, (((1,), (1,)), ((), ())), preferred_element_type=F32)


def mm(a, b):
    return jnp.dot(a, b, preferred_element_type=F32)


def offset_of(k):
    return k + k // 2 - 2 * (k // 3)


def kernel(
    pre_in, dec_in, gain, qbias, kvbias, freq, offset, routing, lens, table,
    wq_hbm, wkv_hbm, wo_hbm, cache_hbm,
    pre_out, dec_out,
    params, x0, x1, wq, wkv, wo, acc0, acc1, ss0, ss1, cos_t, sin_t,
    q0, q1, kvs0, kvs1, kvr0, kvr1, kv, kvd, att0, att1,
    cache, s8, sx, e_own, ex, o8, ox, m_c, l_c, pack, pool, cnt_s, cnt_r, qx, mult,
    tok_slot,
    rs0, rs1,
    w_sem, ag_send, ag_recv, rs_send, rs_recv, pair_send, pair_recv, grp_send, grp_recv,
):
    g = lax.axis_index("group")
    t = lax.axis_index("tp")
    core = g % 2
    y, z = t // 4, t % 4
    f = z + core * (y - z)
    s = y + core * (z - y)

    def tp_of(ff, ss):
        return 4 * ss + ff + core * 3 * (ff - ss)

    fn, fp = tp_of((f + 1) % 4, s), tp_of((f + 3) % 4, s)
    sn, sp = tp_of(f, (s + 1) % 4), tp_of(f, (s + 3) % 4)
    pair = t + 1 - 2 * (t % 2)
    half = t % 2

    drows = dec_in[...].astype(F32)
    drows = jnp.concatenate([drows[0:8], drows[16:24], drows[8:16], drows[24:32]], axis=0)
    first = jnp.concatenate([drows.astype(BF16), pre_in[0:T0]], axis=0)
    x0[0] = first.reshape(2, C0 // 2, FS)
    x1[0] = pre_in[T0:512].reshape(2, C1 // 2, FS)

    barrier = pltpu.get_barrier_semaphore()
    for peer in (fn, fp, sn, sp):
        pl.semaphore_signal(barrier, inc=1, device_id=(g, peer), device_id_type=MESH)
    for j in range(1, 8):
        pl.semaphore_signal(barrier, inc=1, device_id=((g + j) % 8, t), device_id_type=MESH)

    loads = [
        pltpu.make_async_copy(wq_hbm, wq, w_sem.at[0]),
        pltpu.make_async_copy(wkv_hbm, wkv, w_sem.at[1]),
        pltpu.make_async_copy(wo_hbm, wo, w_sem.at[2]),
        pltpu.make_async_copy(cache_hbm, cache, w_sem.at[3]),
    ]
    for load in loads:
        load.start()

    pl.semaphore_wait(barrier, 11)

    def to_tp(src, dst, send, recv, peer):
        return pltpu.make_async_remote_copy(src, dst, send, recv, device_id=(g, peer), device_id_type=MESH)

    class Gather:
        def __init__(self, x, rows, c):
            self.x, self.c, self.sent = x, c, []

        def copy(self, src, dst, part, index, peer):
            src, dst = 4 * src[0] + src[1], 4 * dst[0] + dst[1]
            src = self.x.at[src] if part is None else self.x.at[src, part]
            dst = self.x.at[dst] if part is None else self.x.at[dst, part]
            return to_tp(src, dst, ag_send.at[self.c, index], ag_recv.at[self.c, index], peer)

        def go(self, src, dst, part, index, peer):
            copy = self.copy(src, dst, part, index, peer)
            copy.start()
            self.sent.append(copy)

        def came(self, dst, part, index):
            self.copy(dst, dst, part, index, fn).wait_recv()

        def send_own(self):
            self.go((0, 0), (2, 0), None, 0, fn)
            self.go((0, 0), (1, 0), None, 1, fp)
            self.line(0)

        def line(self, k):
            self.go((k, 0), (k, 2), None, 4 + 4 * k, sn)
            self.go((k, 0), (k, 1), None, 5 + 4 * k, sp)

        def near(self):
            self.came((2, 0), None, 0)
            self.go((2, 0), (3, 0), 0, 2, fn)
            self.line(2)
            self.came((1, 0), None, 1)
            self.go((1, 0), (3, 0), 1, 3, fp)
            self.line(1)

        def far(self):
            self.came((3, 0), 0, 2)
            self.came((3, 0), 1, 3)
            self.line(3)

        def step(self, i):
            j, w = (i - 3) // 3, (i - 3) % 3
            if i < 3:
                if i == 1:
                    self.near()
                return i, 0
            if i == 5:
                self.far()
                return 3, 0
            if i == 15 or w == 2:
                self.came((j - 1, 3), 0, 2 + 4 * j)
                self.came((j - 1, 3), 1, 3 + 4 * j)
                return j - 1, 3
            if w == 0:
                self.came((j, 2), None, 4 + 4 * j)
                self.go((j, 2), (j, 3), 0, 6 + 4 * j, sn)
                return j, 2
            self.came((j, 1), None, 5 + 4 * j)
            self.go((j, 1), (j, 3), 1, 7 + 4 * j, sp)
            return j, 1

        def drain(self):
            for copy in self.sent:
                copy.wait_send()

    ag0, ag1 = Gather(x0, C0, 0), Gather(x1, C1, 1)
    ag0.send_own()
    ag1.send_own()

    def accumulate(x, acc, ss, place):
        kf, ks = place
        slot = tp_of((f + offset_of(kf)) % 4, (s + offset_of(ks)) % 4)
        at = pl.multiple_of(slot * FS, FS)
        xf = x[4 * kf + ks].reshape(-1, FS).astype(F32)
        sq = xf * xf
        ss[...] += sq[:, 0:128] + sq[:, 128:256] + sq[:, 256:384] + sq[:, 384:512]
        xg = (xf * params[pl.ds(slot, 1), :]).astype(BF16)
        acc[:, 0:512] += mm(xg, wq[pl.ds(at, FS), :])
        acc[:, 512:640] += nt(xg, wkv[:, pl.ds(at, FS)])

    for i in range(16):
        params[i:i + 1] = gain[i * FS:(i + 1) * FS].astype(F32).reshape(1, FS)
    params[16:17] = qbias[...].astype(F32).reshape(1, FS)
    params[17:18, 0:HD] = jnp.concatenate([kvbias[0:1].astype(F32), kvbias[1:2].astype(F32)], axis=1)
    acc0[...] = jnp.zeros_like(acc0)
    acc1[...] = jnp.zeros_like(acc1)
    ss0[...] = jnp.zeros_like(ss0)
    ss1[...] = jnp.zeros_like(ss1)
    loads[0].wait()
    loads[1].wait()

    gathers = ((ag0, x0, acc0, ss0), (ag1, x1, acc1, ss1))

    def advance(c, *steps):
        ag, x, acc, ss = gathers[c]
        for place in [ag.step(i) for i in steps]:
            accumulate(x, acc, ss, place)

    advance(0, 0, 1, 2, 3, 4)
    advance(0, 5)

    advance(1, 0, 1, 2, 3, 4)
    advance(0, 6, 7, 8)
    advance(1, 5)
    advance(0, 9, 10, 11)
    advance(1, 6, 7, 8)
    advance(0, 12, 13)

    lane = lax.broadcasted_iota(jnp.int32, (C0, HD), 1)
    row = lax.broadcasted_iota(jnp.int32, (C0, HD), 0)
    places = row - DEC + offset[0]
    for r in range(16):
        base = (r // 8) * 16 + r % 8
        places = jnp.where(row == base, lens[r], places)
        places = jnp.where(row == base + 8, lens[r] + 1, places)
    sign = jnp.where(lane < 64, -1.0, 1.0).astype(F32)
    angle = places.astype(F32) * freq[...]
    cos_t[0:C0] = jnp.cos(angle)
    sin_t[0:C0] = jnp.sin(angle) * sign
    row = lax.broadcasted_iota(jnp.int32, (C1, HD), 0)
    angle = (row + (T0 + offset[0])).astype(F32) * freq[...]
    cos_t[C0:C0 + C1] = jnp.cos(angle)
    sin_t[C0:C0 + C1] = jnp.sin(angle) * sign[0:1]

    token = lax.broadcasted_iota(jnp.int32, (8, 512), 1)

    def rank_block(b, carry):
        slots, counts = carry
        d = routing[b]
        rank = jnp.int32(0)
        for k in range(8):
            rank = rank + jnp.where(d == k, counts[k], 0)
        slots = jnp.where(token // 16 == b, d * 128 + rank * 16 + token % 16, slots)
        return slots, tuple(counts[k] + jnp.where(d == k, 1, 0) for k in range(8))

    slots, counts = lax.fori_loop(
        0, 32, rank_block, (jnp.zeros((8, 512), jnp.int32), (jnp.int32(0),) * 8)
    )
    tok_slot[...] = slots
    for k in range(8):
        cnt_s[k] = jnp.full((8, 128), 1.0, F32) * counts[k].astype(F32)

    page = lax.broadcasted_iota(jnp.int32, (16, 1024), 1) // 16
    prow = lax.broadcasted_iota(jnp.int32, (16, 1024), 0)

    def count_pages(i, times):
        r, j = i // 8, i % 8
        return times + jnp.where((prow == r) & (page == table[j, r]), 1.0, 0.0)

    mult[...] = lax.fori_loop(0, 128, count_pages, jnp.zeros((16, 1024), F32))

    advance(0, 14, 15)

    def finish(acc, ss, kvs, q, table_at, rows):
        inv = lax.rsqrt(jnp.sum(ss[...], axis=1, keepdims=True) * (1.0 / WIDTH) + EPSILON)
        kvs[...] = (acc[:, 512:640] * inv + params[17:18, 0:HD]).astype(BF16)
        return inv

    def finish_q(acc, ss, q, table_at, rows):
        inv = lax.rsqrt(jnp.sum(ss[...], axis=1, keepdims=True) * (1.0 / WIDTH) + EPSILON)
        c, sn_ = cos_t[table_at:table_at + rows], sin_t[table_at:table_at + rows]
        for h in range(4):
            at = slice(h * HD, (h + 1) * HD)
            v = acc[:, at] * inv + params[16:17, at]
            q[:, at] = (v * c + pltpu.roll(v, 64, 1) * sn_).astype(BF16)

    def join(own, other, table_at, rows):
        a, b = own[...].astype(F32), other[...].astype(F32)
        lo = jnp.where(half == 0, a, b)
        hi = jnp.where(half == 0, b, a)
        low = lax.broadcasted_iota(jnp.int32, (rows, HD), 1) < 64
        k = jnp.where(low, lo, pltpu.roll(hi, 64, 1))
        v = jnp.where(low, pltpu.roll(lo, 64, 1), hi)
        k = k * cos_t[table_at:table_at + rows] + pltpu.roll(k, 64, 1) * sin_t[table_at:table_at + rows]
        return k.astype(BF16), v.astype(BF16)

    def pair_copy(src, dst, index):
        return to_tp(src, dst, pair_send.at[index], pair_recv.at[index], pair)

    kv_join = [pair_copy(kvs0, kvr0, 0), pair_copy(kvs1, kvr1, 1)]
    q_swap = pair_copy(q0.at[pl.ds(0, DEC)], qx, 2)
    s_swap = pair_copy(s8.at[pl.ds(HD, HD)], sx, 3)
    e_swap = pair_copy(e_own, ex, 4)
    o_swap = pair_copy(o8.at[pl.ds(HD, HD)], ox, 5)

    scale = HD ** (-0.5)

    def attend(q, start, rows, att, h, keys):
        at = pl.ds(h * HD, HD)
        sc = nt(q[start:start + rows, at], kv[0:keys, 0:HD]) * scale
        qi = lax.broadcasted_iota(jnp.int32, (rows, keys), 0) + (keys - rows)
        ki = lax.broadcasted_iota(jnp.int32, (rows, keys), 1)
        sc = jnp.where(ki <= qi, sc, NEG_FILL)
        e = jnp.exp(sc - jnp.max(sc, axis=1, keepdims=True))
        total = jnp.sum(e, axis=1, keepdims=True)
        att[0:rows, at] = (mm(e.astype(BF16), kv[0:keys, HD:2 * HD]) / total).astype(BF16)

    def query_row(shape):
        m = lax.broadcasted_iota(jnp.int32, shape, 0)
        return m % DEC // 16 * 8 + m % 8

    def by_head(ref):
        return jnp.concatenate([ref[0:DEC, h * HD:(h + 1) * HD] for h in range(4)], axis=0)

    def padded(part):
        zero = jnp.zeros((64, CACHE), BF16)
        return jnp.where(half == 0, jnp.concatenate([part, zero], axis=0), jnp.concatenate([zero, part], axis=0))

    def cache_scores():
        q_swap.wait_recv()
        loads[3].wait()
        q8 = jnp.concatenate([by_head(q0), by_head(qx)], axis=0)
        s8[...] = jnp.zeros_like(s8)

        @pl.loop(0, 16)
        def _(r):
            s8[...] = jnp.where(query_row((256, CACHE)) == r, mm(q8, padded(cache[r, 0])), s8[...])

        s_swap.start()

    def cache_weights():
        s_swap.wait_recv()
        owner = query_row((HD, CACHE))
        length = jnp.zeros((HD, CACHE), jnp.int32)
        for r in range(16):
            length = jnp.where(owner == r, lens[r], length)
        sc = (s8[0:HD] + sx[...]) * scale
        sc = jnp.where(lax.broadcasted_iota(jnp.int32, (HD, CACHE), 1) < length, sc, NEG_FILL)
        top = jnp.max(sc, axis=1, keepdims=True)
        e = jnp.exp(sc - top)
        m_c[...] = jnp.broadcast_to(top, (HD, HD))
        l_c[...] = jnp.broadcast_to(jnp.sum(e, axis=1, keepdims=True), (HD, HD))
        e_own[...] = e.astype(BF16)
        e_swap.start()

    def cache_values():
        e_swap.wait_recv()
        e8 = jnp.concatenate([e_own[...], ex[...]], axis=0)
        o8[...] = jnp.zeros_like(o8)

        @pl.loop(0, 16)
        def _(r):
            o8[...] = jnp.where(query_row((256, HD)) == r, nt(e8, padded(cache[r, 1])), o8[...])

        o_swap.start()

    def pass_keys(c, kvs, kvr, at, rows):
        kv_join[c].wait_recv()
        k, v = join(kvs, kvr, at, rows)
        if c == 0:
            kvd[:, 0:HD] = k[0:DEC]
            kvd[:, HD:2 * HD] = v[0:DEC]
            k, v = k[DEC:C0], v[DEC:C0]
        tokens = slice(0, T0) if c == 0 else slice(T0, 512)
        kv[tokens, 0:HD] = k
        kv[tokens, HD:2 * HD] = v

    class Scatter:
        def __init__(self, bufs, att, rows, c):
            (self.s1, self.ra, self.rb, self.s2p, self.s2m, self.rm, self.rp,
             self.s3, self.fa, self.fb, self.gm, self.gp) = bufs
            self.att, self.c = att, c
            self.up = (pl.ds(0, rows // 2), slice(None))
            self.lo = (pl.ds(rows // 2, rows // 2), slice(None))

        def term(self, kf, ks):
            slot = tp_of((f + offset_of(kf)) % 4, (s + offset_of(ks)) % 4)
            return mm(self.att[...], wo[:, pl.ds(pl.multiple_of(slot * FS, FS), FS)])

        def copy(self, src, dst, index, peer):
            return to_tp(src, dst, rs_send.at[self.c, index], rs_recv.at[self.c, index], peer)

        def merge(self, p, part, upper):
            axis = 0
            n = p.shape[axis] // 2
            a, b = lax.slice_in_dim(p, 0, n, axis=axis), lax.slice_in_dim(p, n, 2 * n, axis=axis)
            if upper:
                a = a + part.astype(F32)
            else:
                b = b + part.astype(F32)
            return jnp.concatenate([a, b], axis=axis).astype(BF16)

        def upper(self, k):
            return self.copy(self.s1.at[(k, *self.up)], self.ra.at[k], 4 * k, sn)

        def lower(self, k):
            return self.copy(self.s1.at[(k, *self.lo)], self.rb.at[k], 4 * k + 1, sp)

        def ahead(self, k):
            return self.copy(self.s2p.at[k], self.rm.at[k], 4 * k + 2, sn)

        def back(self, k):
            return self.copy(self.s2m.at[k], self.rp.at[k], 4 * k + 3, sp)

        def last(self):
            return [
                self.copy(self.s3.at[(0, *self.up)], self.fa, 16, fn),
                self.copy(self.s3.at[(0, *self.lo)], self.fb, 17, fp),
                self.copy(self.s3.at[1], self.gm, 18, fn),
                self.copy(self.s3.at[2], self.gp, 19, fp),
            ]

        def first_hop(self):
            @pl.loop(0, 4)
            def _(j):
                k = 3 - j
                self.s1[k] = self.term(k, 3).astype(BF16)
                self.upper(k).start()
                self.lower(k).start()

        def second_hop(self):
            @pl.loop(0, 4)
            def _(j):
                k = 3 - j
                p = self.term(k, 1)
                self.upper(k).wait_recv()
                self.s2p[k] = self.merge(p, self.ra[k], True)
                self.ahead(k).start()
                p = self.term(k, 2)
                self.lower(k).wait_recv()
                self.s2m[k] = self.merge(p, self.rb[k], False)
                self.back(k).start()

        def gathered(self, k):
            p = self.term(k, 0)
            self.ahead(k).wait_recv()
            self.back(k).wait_recv()
            return p + self.rm[k].astype(F32) + self.rp[k].astype(F32)

        def third_hop(self):
            c1, c2, c3, c4 = self.last()
            self.s3[0] = self.gathered(3).astype(BF16)
            c1.start()
            c2.start()
            p = self.gathered(1)
            c1.wait_recv()
            self.s3[1] = self.merge(p, self.fa[...], True)
            c3.start()
            p = self.gathered(2)
            c2.wait_recv()
            self.s3[2] = self.merge(p, self.fb[...], False)
            c4.start()

        def result(self):
            _, _, c3, c4 = self.last()
            p = self.gathered(0)
            c3.wait_recv()
            c4.wait_recv()
            return p + self.gm[...].astype(F32) + self.gp[...].astype(F32)

        def drain(self):
            for k in range(4):
                for c in (self.upper(k), self.lower(k), self.ahead(k), self.back(k)):
                    c.wait_send()
            for c in self.last():
                c.wait_send()

    sc0, sc1 = Scatter(rs0, att0, T0, 0), Scatter(rs1, att1, T1 + DEC, 1)

    def group_copies(j):
        there = (g + j) % 8
        dev = (there, t)
        return (
            pltpu.make_async_remote_copy(pack.at[j], pool.at[j], grp_send.at[0, j], grp_recv.at[0, j],
                                         device_id=dev, device_id_type=MESH),
            pltpu.make_async_remote_copy(cnt_s.at[there], cnt_r.at[j], grp_send.at[1, j], grp_recv.at[1, j],
                                         device_id=dev, device_id_type=MESH),
        )

    def send_pages():
        @pl.loop(0, 8)
        def _(j):
            there = (g + j) % 8
            want = lax.broadcasted_iota(jnp.int32, (128, 512), 0) + there * 128
            hot = jnp.where(tok_slot[0:1, :] == want, 1.0, 0.0).astype(BF16)
            pages = mm(hot, kv[...]).astype(BF16)

            @pl.when(j == 0)
            def _():
                pool[0] = pages
                cnt_r[0] = cnt_s[there]

            @pl.when(j > 0)
            def _():
                pack[j] = pages
                for c in group_copies(j):
                    c.start()

    def decode_rows():
        @pl.loop(1, 8)
        def _(j):
            for c in group_copies(j):
                c.wait_recv()

        qa = by_head(q0)
        scores, weight = [], []
        for src in range(8):
            sc = nt(qa, pool[src, :, 0:HD]) * scale
            slot = lax.broadcasted_iota(jnp.int32, (16, HD), 1) // 16
            at = pl.multiple_of((g + 8 - src) % 8 * HD, HD)
            m16 = jnp.where(slot.astype(F32) < cnt_r[src, 0:1], mult[:, pl.ds(at, HD)], 0.0)
            m = jnp.concatenate([m16[0:8], m16[0:8], m16[8:16], m16[8:16]] * 4, axis=0)
            weight.append(m)
            scores.append(jnp.where(m > 0.0, sc, NEG_FILL))
        new = jnp.concatenate([kvd[...], jnp.zeros((HD - DEC, 2 * HD), BF16)], axis=0)
        col = lax.broadcasted_iota(jnp.int32, (HD, HD), 1)
        same = (col // 16 * 8 + col % 8 == query_row((HD, HD))) & (col < DEC)
        step = lax.broadcasted_iota(jnp.int32, (HD, HD), 0) // 8 % 2
        ok = same & (col // 8 % 2 <= step)
        scores.append(jnp.where(ok, nt(qa, new[:, 0:HD]) * scale, NEG_FILL))
        top = m_c[...]
        for sc in scores:
            top = jnp.maximum(top, jnp.max(sc, axis=1, keepdims=True))
        o_swap.wait_recv()
        old = jnp.exp(m_c[...] - top)
        total = l_c[...] * old
        mixed = (o8[0:HD] + ox[...]) * old
        for i in range(9):
            e = jnp.exp(scores[i] - top)
            if i < 8:
                e = e * weight[i]
            total = total + jnp.sum(e, axis=1, keepdims=True)
            values = pool[i, :, HD:2 * HD] if i < 8 else new[:, HD:2 * HD]
            mixed = mixed + mm(e.astype(BF16), values)
        mixed = (mixed / total).astype(BF16)
        for h in range(4):
            att1[T1:T1 + DEC, h * HD:(h + 1) * HD] = mixed[h * DEC:(h + 1) * DEC]

    finish(acc0, ss0, kvs0, q0, 0, C0)
    kv_join[0].start()
    finish_q(acc0, ss0, q0, 0, C0)
    q_swap.start()
    advance(1, 9, 10, 11)
    pass_keys(0, kvs0, kvr0, 0, C0)
    for h in range(4):
        attend(q0, DEC, T0, att0, h, T0)
    loads[2].wait()
    sc0.first_hop()
    advance(1, 12, 13)
    cache_scores()
    advance(1, 14, 15)
    finish(acc1, ss1, kvs1, q1, C0, C1)
    kv_join[1].start()
    cache_weights()
    finish_q(acc1, ss1, q1, C0, C1)
    sc0.second_hop()
    pass_keys(1, kvs1, kvr1, C0, C1)
    send_pages()
    cache_values()
    for h in range(4):
        attend(q1, 0, T1, att1, h, 512)
    sc0.third_hop()
    decode_rows()
    sc1.first_hop()
    sc1.second_hop()
    pre_out[0:T0] = (sc0.result() + pre_in[0:T0].astype(F32)).astype(BF16)
    sc1.third_hop()
    last = sc1.result()
    pre_out[T0:512] = (last[0:T1] + pre_in[T0:512].astype(F32)).astype(BF16)
    dsum = last[T1:T1 + DEC]
    dsum = jnp.concatenate([dsum[0:8], dsum[16:24], dsum[8:16], dsum[24:32]], axis=0)
    dec_out[...] = (dsum + dec_in[...].astype(F32)).astype(BF16)

    ag0.drain()
    ag1.drain()
    sc0.drain()
    sc1.drain()
    for c in kv_join + [q_swap, s_swap, e_swap, o_swap]:
        c.wait_send()

    @pl.loop(1, 8)
    def _(j):
        for c in group_copies(j):
            c.wait_send()


def scatter_bufs(rows):
    h, w = rows // 2, FS
    return (
        pltpu.VMEM((4, rows, FS), BF16),
        pltpu.VMEM((4, h, w), BF16),
        pltpu.VMEM((4, h, w), BF16),
        pltpu.VMEM((4, rows, FS), BF16),
        pltpu.VMEM((4, rows, FS), BF16),
        pltpu.VMEM((4, rows, FS), BF16),
        pltpu.VMEM((4, rows, FS), BF16),
        pltpu.VMEM((3, rows, FS), BF16),
        pltpu.VMEM((h, w), BF16),
        pltpu.VMEM((h, w), BF16),
        pltpu.VMEM((rows, FS), BF16),
        pltpu.VMEM((rows, FS), BF16),
    )


def body(
    prefill_in, decode_in, norm_gain, query_weight, query_bias, keyval_weight, keyval_bias,
    out_weight, pass_offset, routing, cache_len, page_table, cache_keyval,
):
    half_lanes = np.arange(HD) % 64
    freq = jnp.asarray((1000000.0 ** (-(half_lanes * (2.0 / HD)))).astype(np.float32).reshape(1, HD))
    vmem = pl.BlockSpec(memory_space=pltpu.VMEM)
    smem = pl.BlockSpec(memory_space=pltpu.SMEM)
    hbm = pl.BlockSpec(memory_space=pl.ANY)
    pre, dec = pl.pallas_call(
        kernel,
        out_shape=(
            jax.ShapeDtypeStruct((512, FS), BF16),
            jax.ShapeDtypeStruct((DEC, FS), BF16),
        ),
        in_specs=[vmem] * 6 + [smem] * 4 + [hbm] * 4,
        out_specs=(vmem, vmem),
        scratch_shapes=[
            pltpu.VMEM((18, FS), F32),
            pltpu.VMEM((16, 2, C0 // 2, FS), BF16),
            pltpu.VMEM((16, 2, C1 // 2, FS), BF16),
            pltpu.VMEM((WIDTH, FS), BF16),
            pltpu.VMEM((HD, WIDTH), BF16),
            pltpu.VMEM((FS, WIDTH), BF16),
            pltpu.VMEM((C0, 640), F32),
            pltpu.VMEM((C1, 640), F32),
            pltpu.VMEM((C0, HD), F32),
            pltpu.VMEM((C1, HD), F32),
            pltpu.VMEM((C0 + C1, HD), F32),
            pltpu.VMEM((C0 + C1, HD), F32),
            pltpu.VMEM((C0, FS), BF16),
            pltpu.VMEM((C1, FS), BF16),
            pltpu.VMEM((C0, HD), BF16),
            pltpu.VMEM((C1, HD), BF16),
            pltpu.VMEM((C0, HD), BF16),
            pltpu.VMEM((C1, HD), BF16),
            pltpu.VMEM((512, 2 * HD), BF16),
            pltpu.VMEM((DEC, 2 * HD), BF16),
            pltpu.VMEM((T0, FS), BF16),
            pltpu.VMEM((T1 + DEC, FS), BF16),
            pltpu.VMEM((16, 2, 64, CACHE), BF16),
            pltpu.VMEM((256, CACHE), F32),
            pltpu.VMEM((HD, CACHE), F32),
            pltpu.VMEM((HD, CACHE), BF16),
            pltpu.VMEM((HD, CACHE), BF16),
            pltpu.VMEM((256, HD), F32),
            pltpu.VMEM((HD, HD), F32),
            pltpu.VMEM((HD, HD), F32),
            pltpu.VMEM((HD, HD), F32),
            pltpu.VMEM((8, HD, 2 * HD), BF16),
            pltpu.VMEM((8, HD, 2 * HD), BF16),
            pltpu.VMEM((8, 8, HD), F32),
            pltpu.VMEM((8, 8, HD), F32),
            pltpu.VMEM((DEC, FS), BF16),
            pltpu.VMEM((16, 1024), F32),
            pltpu.VMEM((8, 512), jnp.int32),
            scatter_bufs(T0),
            scatter_bufs(T1 + DEC),
            pltpu.SemaphoreType.DMA((4,)),
            pltpu.SemaphoreType.DMA((2, 20)),
            pltpu.SemaphoreType.DMA((2, 20)),
            pltpu.SemaphoreType.DMA((3, 20)),
            pltpu.SemaphoreType.DMA((3, 20)),
            pltpu.SemaphoreType.DMA((6,)),
            pltpu.SemaphoreType.DMA((6,)),
            pltpu.SemaphoreType.DMA((2, 8)),
            pltpu.SemaphoreType.DMA((2, 8)),
        ],
        compiler_params=pltpu.CompilerParams(
            collective_id=0, has_side_effects=True, vmem_limit_bytes=62 * 2**20
        ),
    )(
        prefill_in,
        decode_in.reshape(DEC, FS),
        norm_gain,
        query_bias,
        keyval_bias,
        freq,
        pass_offset,
        routing.reshape(32),
        cache_len,
        page_table.T,
        query_weight,
        keyval_weight.transpose(1, 2, 0).reshape(HD, WIDTH),
        out_weight,
        cache_keyval.transpose(0, 2, 3, 1),
    )
    return pre, dec.reshape(2, 16, FS)


def solution(mesh):
    in_specs = (
        P("group", "tp"),
        P(None, "group", "tp"),
        P(),
        P(None, "tp"),
        P("tp"),
        P(None, None, "tp"),
        P(None, "tp"),
        P("tp", None),
        P("group"),
        P("group", None),
        P("group"),
        P("group", None),
        P("group", None, None, "tp"),
    )
    out_specs = (P("group", "tp"), P(None, "group", "tp"))
    return jax.shard_map(body, mesh=mesh, in_specs=in_specs, out_specs=out_specs, check_vma=False)
```

```python
import jax
import jax.numpy as jnp
import numpy as np
from jax import lax
from jax.experimental import pallas as pl
from jax.experimental.pallas import tpu as pltpu
from jax.sharding import PartitionSpec as P

MESH = pl.DeviceIdType.MESH
F32 = jnp.float32
BF16 = jnp.bfloat16
HD = 128
FS = 512
DEC = 32
T0, T1 = 256, 256
C0, C1 = DEC + T0, T1
NEG_FILL = -1e30
EPSILON = 1e-06
CACHE = 256
WIDTH = 8192


def nt(a, b):
    return lax.dot_general(a, b, (((1,), (1,)), ((), ())), preferred_element_type=F32)


def mm(a, b):
    return jnp.dot(a, b, preferred_element_type=F32)


def offset_of(k):
    return k + k // 2 - 2 * (k // 3)


def kernel(
    pre_in, dec_in, gain, qbias, kvbias, freq, offset, routing, lens, table,
    wq_hbm, wkv_hbm, wo_hbm, cache_hbm,
    pre_out, dec_out,
    params, x0, x1, wq, wkv, wo, acc0, acc1, ss0, ss1, cos_t, sin_t,
    q0, q1, kvs0, kvs1, kvr0, kvr1, kv, kvd, att0, att1,
    cache, s8, sx, e_own, ex, o8, ox, m_c, l_c, pack, pool, cnt_s, cnt_r, qx, mult,
    tok_slot,
    rs0, rs1,
    w_sem, ag_send, ag_recv, rs_send, rs_recv, pair_send, pair_recv, grp_send, grp_recv,
):
    g = lax.axis_index("group")
    t = lax.axis_index("tp")
    core = g % 2
    y, z = t // 4, t % 4
    f = z + core * (y - z)
    s = y + core * (z - y)

    def tp_of(ff, ss):
        return 4 * ss + ff + core * 3 * (ff - ss)

    fn, fp = tp_of((f + 1) % 4, s), tp_of((f + 3) % 4, s)
    sn, sp = tp_of(f, (s + 1) % 4), tp_of(f, (s + 3) % 4)
    pair = t + 1 - 2 * (t % 2)
    half = t % 2

    drows = dec_in[...].astype(F32)
    drows = jnp.concatenate([drows[0:8], drows[16:24], drows[8:16], drows[24:32]], axis=0)
    first = jnp.concatenate([drows.astype(BF16), pre_in[0:T0]], axis=0)
    x0[0] = first.reshape(2, C0 // 2, FS)
    x1[0] = pre_in[T0:512].reshape(2, C1 // 2, FS)

    barrier = pltpu.get_barrier_semaphore()
    for peer in (fn, fp, sn, sp):
        pl.semaphore_signal(barrier, inc=1, device_id=(g, peer), device_id_type=MESH)
    for j in range(1, 8):
        pl.semaphore_signal(barrier, inc=1, device_id=((g + j) % 8, t), device_id_type=MESH)

    loads = [
        pltpu.make_async_copy(wq_hbm, wq, w_sem.at[0]),
        pltpu.make_async_copy(wkv_hbm, wkv, w_sem.at[1]),
        pltpu.make_async_copy(wo_hbm, wo, w_sem.at[2]),
        pltpu.make_async_copy(cache_hbm, cache, w_sem.at[3]),
    ]
    for load in loads:
        load.start()

    pl.semaphore_wait(barrier, 11)

    def to_tp(src, dst, send, recv, peer):
        return pltpu.make_async_remote_copy(src, dst, send, recv, device_id=(g, peer), device_id_type=MESH)

    class Gather:
        def __init__(self, x, rows, c):
            self.x, self.c, self.sent = x, c, []

        def copy(self, src, dst, part, index, peer):
            src, dst = 4 * src[0] + src[1], 4 * dst[0] + dst[1]
            src = self.x.at[src] if part is None else self.x.at[src, part]
            dst = self.x.at[dst] if part is None else self.x.at[dst, part]
            return to_tp(src, dst, ag_send.at[self.c, index], ag_recv.at[self.c, index], peer)

        def go(self, src, dst, part, index, peer):
            copy = self.copy(src, dst, part, index, peer)
            copy.start()
            self.sent.append(copy)

        def came(self, dst, part, index):
            self.copy(dst, dst, part, index, fn).wait_recv()

        def send_own(self):
            self.go((0, 0), (2, 0), None, 0, fn)
            self.go((0, 0), (1, 0), None, 1, fp)
            self.line(0)

        def line(self, k):
            self.go((k, 0), (k, 2), None, 4 + 4 * k, sn)
            self.go((k, 0), (k, 1), None, 5 + 4 * k, sp)

        def near(self):
            self.came((2, 0), None, 0)
            self.go((2, 0), (3, 0), 0, 2, fn)
            self.line(2)
            self.came((1, 0), None, 1)
            self.go((1, 0), (3, 0), 1, 3, fp)
            self.line(1)

        def far(self):
            self.came((3, 0), 0, 2)
            self.came((3, 0), 1, 3)
            self.line(3)

        def step(self, i):
            j, w = (i - 3) // 3, (i - 3) % 3
            if i < 3:
                if i == 1:
                    self.near()
                return i, 0
            if i == 5:
                self.far()
                return 3, 0
            if i == 15 or w == 2:
                self.came((j - 1, 3), 0, 2 + 4 * j)
                self.came((j - 1, 3), 1, 3 + 4 * j)
                return j - 1, 3
            if w == 0:
                self.came((j, 2), None, 4 + 4 * j)
                self.go((j, 2), (j, 3), 0, 6 + 4 * j, sn)
                return j, 2
            self.came((j, 1), None, 5 + 4 * j)
            self.go((j, 1), (j, 3), 1, 7 + 4 * j, sp)
            return j, 1

        def drain(self):
            for copy in self.sent:
                copy.wait_send()

    ag0, ag1 = Gather(x0, C0, 0), Gather(x1, C1, 1)
    ag0.send_own()
    ag1.send_own()

    def accumulate(x, acc, ss, place):
        kf, ks = place
        slot = tp_of((f + offset_of(kf)) % 4, (s + offset_of(ks)) % 4)
        at = pl.multiple_of(slot * FS, FS)
        xf = x[4 * kf + ks].reshape(-1, FS).astype(F32)
        sq = xf * xf
        ss[...] += sq[:, 0:128] + sq[:, 128:256] + sq[:, 256:384] + sq[:, 384:512]
        xg = (xf * params[pl.ds(slot, 1), :]).astype(BF16)
        acc[:, 0:512] += mm(xg, wq[pl.ds(at, FS), :])
        acc[:, 512:640] += nt(xg, wkv[:, pl.ds(at, FS)])

    for i in range(16):
        params[i:i + 1] = gain[i * FS:(i + 1) * FS].astype(F32).reshape(1, FS)
    params[16:17] = qbias[...].astype(F32).reshape(1, FS)
    params[17:18, 0:HD] = jnp.concatenate([kvbias[0:1].astype(F32), kvbias[1:2].astype(F32)], axis=1)
    acc0[...] = jnp.zeros_like(acc0)
    acc1[...] = jnp.zeros_like(acc1)
    ss0[...] = jnp.zeros_like(ss0)
    ss1[...] = jnp.zeros_like(ss1)
    loads[0].wait()
    loads[1].wait()

    gathers = ((ag0, x0, acc0, ss0), (ag1, x1, acc1, ss1))

    def advance(c, *steps):
        ag, x, acc, ss = gathers[c]
        for place in [ag.step(i) for i in steps]:
            accumulate(x, acc, ss, place)

    advance(0, 0, 1, 2, 3, 4)
    advance(0, 5)

    advance(1, 0, 1, 2, 3, 4)
    advance(0, 6, 7, 8)
    advance(1, 5)
    advance(0, 9, 10, 11)
    advance(1, 6, 7, 8)
    advance(0, 12, 13)

    lane = lax.broadcasted_iota(jnp.int32, (C0, HD), 1)
    row = lax.broadcasted_iota(jnp.int32, (C0, HD), 0)
    places = row - DEC + offset[0]
    for r in range(16):
        base = (r // 8) * 16 + r % 8
        places = jnp.where(row == base, lens[r], places)
        places = jnp.where(row == base + 8, lens[r] + 1, places)
    sign = jnp.where(lane < 64, -1.0, 1.0).astype(F32)
    angle = places.astype(F32) * freq[...]
    cos_t[0:C0] = jnp.cos(angle)
    sin_t[0:C0] = jnp.sin(angle) * sign
    row = lax.broadcasted_iota(jnp.int32, (C1, HD), 0)
    angle = (row + (T0 + offset[0])).astype(F32) * freq[...]
    cos_t[C0:C0 + C1] = jnp.cos(angle)
    sin_t[C0:C0 + C1] = jnp.sin(angle) * sign[0:1]

    token = lax.broadcasted_iota(jnp.int32, (8, 512), 1)

    def rank_block(b, carry):
        slots, counts = carry
        d = routing[b]
        rank = jnp.int32(0)
        for k in range(8):
            rank = rank + jnp.where(d == k, counts[k], 0)
        slots = jnp.where(token // 16 == b, d * 128 + rank * 16 + token % 16, slots)
        return slots, tuple(counts[k] + jnp.where(d == k, 1, 0) for k in range(8))

    slots, counts = lax.fori_loop(
        0, 32, rank_block, (jnp.zeros((8, 512), jnp.int32), (jnp.int32(0),) * 8)
    )
    tok_slot[...] = slots
    for k in range(8):
        cnt_s[k] = jnp.full((8, 128), 1.0, F32) * counts[k].astype(F32)

    page = lax.broadcasted_iota(jnp.int32, (16, 1024), 1) // 16
    prow = lax.broadcasted_iota(jnp.int32, (16, 1024), 0)

    def count_pages(i, times):
        r, j = i // 8, i % 8
        return times + jnp.where((prow == r) & (page == table[j, r]), 1.0, 0.0)

    mult[...] = lax.fori_loop(0, 128, count_pages, jnp.zeros((16, 1024), F32))

    advance(0, 14, 15)

    def finish(acc, ss, kvs, q, table_at, rows):
        inv = lax.rsqrt(jnp.sum(ss[...], axis=1, keepdims=True) * (1.0 / WIDTH) + EPSILON)
        kvs[...] = (acc[:, 512:640] * inv + params[17:18, 0:HD]).astype(BF16)
        return inv

    def finish_q(acc, ss, q, table_at, rows):
        inv = lax.rsqrt(jnp.sum(ss[...], axis=1, keepdims=True) * (1.0 / WIDTH) + EPSILON)
        c, sn_ = cos_t[table_at:table_at + rows], sin_t[table_at:table_at + rows]
        for h in range(4):
            at = slice(h * HD, (h + 1) * HD)
            v = acc[:, at] * inv + params[16:17, at]
            q[:, at] = (v * c + pltpu.roll(v, 64, 1) * sn_).astype(BF16)

    def join(own, other, table_at, rows):
        a, b = own[...].astype(F32), other[...].astype(F32)
        lo = jnp.where(half == 0, a, b)
        hi = jnp.where(half == 0, b, a)
        low = lax.broadcasted_iota(jnp.int32, (rows, HD), 1) < 64
        k = jnp.where(low, lo, pltpu.roll(hi, 64, 1))
        v = jnp.where(low, pltpu.roll(lo, 64, 1), hi)
        k = k * cos_t[table_at:table_at + rows] + pltpu.roll(k, 64, 1) * sin_t[table_at:table_at + rows]
        return k.astype(BF16), v.astype(BF16)

    def pair_copy(src, dst, index):
        return to_tp(src, dst, pair_send.at[index], pair_recv.at[index], pair)

    kv_join = [pair_copy(kvs0, kvr0, 0), pair_copy(kvs1, kvr1, 1)]
    q_swap = pair_copy(q0.at[pl.ds(0, DEC)], qx, 2)
    s_swap = pair_copy(s8.at[pl.ds(HD, HD)], sx, 3)
    e_swap = pair_copy(e_own, ex, 4)
    o_swap = pair_copy(o8.at[pl.ds(HD, HD)], ox, 5)

    scale = HD ** (-0.5)

    def attend(q, start, rows, att, h, keys):
        at = pl.ds(h * HD, HD)
        sc = nt(q[start:start + rows, at], kv[0:keys, 0:HD]) * scale
        qi = lax.broadcasted_iota(jnp.int32, (rows, keys), 0) + (keys - rows)
        ki = lax.broadcasted_iota(jnp.int32, (rows, keys), 1)
        sc = jnp.where(ki <= qi, sc, NEG_FILL)
        e = jnp.exp(sc - jnp.max(sc, axis=1, keepdims=True))
        total = jnp.sum(e, axis=1, keepdims=True)
        att[0:rows, at] = (mm(e.astype(BF16), kv[0:keys, HD:2 * HD]) / total).astype(BF16)

    def query_row(shape):
        m = lax.broadcasted_iota(jnp.int32, shape, 0)
        return m % DEC // 16 * 8 + m % 8

    def by_head(ref):
        return jnp.concatenate([ref[0:DEC, h * HD:(h + 1) * HD] for h in range(4)], axis=0)

    def padded(part):
        zero = jnp.zeros((64, CACHE), BF16)
        return jnp.where(half == 0, jnp.concatenate([part, zero], axis=0), jnp.concatenate([zero, part], axis=0))

    def cache_scores():
        q_swap.wait_recv()
        loads[3].wait()
        q8 = jnp.concatenate([by_head(q0), by_head(qx)], axis=0)
        s8[...] = jnp.zeros_like(s8)

        @pl.loop(0, 16)
        def _(r):
            s8[...] = jnp.where(query_row((256, CACHE)) == r, mm(q8, padded(cache[r, 0])), s8[...])

        s_swap.start()

    def cache_weights():
        s_swap.wait_recv()
        owner = query_row((HD, CACHE))
        length = jnp.zeros((HD, CACHE), jnp.int32)
        for r in range(16):
            length = jnp.where(owner == r, lens[r], length)
        sc = (s8[0:HD] + sx[...]) * scale
        sc = jnp.where(lax.broadcasted_iota(jnp.int32, (HD, CACHE), 1) < length, sc, NEG_FILL)
        top = jnp.max(sc, axis=1, keepdims=True)
        e = jnp.exp(sc - top)
        m_c[...] = jnp.broadcast_to(top, (HD, HD))
        l_c[...] = jnp.broadcast_to(jnp.sum(e, axis=1, keepdims=True), (HD, HD))
        e_own[...] = e.astype(BF16)
        e_swap.start()

    def cache_values():
        e_swap.wait_recv()
        e8 = jnp.concatenate([e_own[...], ex[...]], axis=0)
        o8[...] = jnp.zeros_like(o8)

        @pl.loop(0, 16)
        def _(r):
            o8[...] = jnp.where(query_row((256, HD)) == r, nt(e8, padded(cache[r, 1])), o8[...])

        o_swap.start()

    def pass_keys(c, kvs, kvr, at, rows):
        kv_join[c].wait_recv()
        k, v = join(kvs, kvr, at, rows)
        if c == 0:
            kvd[:, 0:HD] = k[0:DEC]
            kvd[:, HD:2 * HD] = v[0:DEC]
            k, v = k[DEC:C0], v[DEC:C0]
        tokens = slice(0, T0) if c == 0 else slice(T0, 512)
        kv[tokens, 0:HD] = k
        kv[tokens, HD:2 * HD] = v

    class Scatter:
        def __init__(self, bufs, att, rows, c):
            (self.s1, self.ra, self.rb, self.s2p, self.s2m, self.rm, self.rp,
             self.s3, self.fa, self.fb, self.gm, self.gp) = bufs
            self.att, self.c = att, c
            self.up = (pl.ds(0, rows // 2), slice(None))
            self.lo = (pl.ds(rows // 2, rows // 2), slice(None))

        def term(self, kf, ks):
            slot = tp_of((f + offset_of(kf)) % 4, (s + offset_of(ks)) % 4)
            return mm(self.att[...], wo[:, pl.ds(pl.multiple_of(slot * FS, FS), FS)])

        def copy(self, src, dst, index, peer):
            return to_tp(src, dst, rs_send.at[self.c, index], rs_recv.at[self.c, index], peer)

        def merge(self, p, part, upper):
            axis = 0
            n = p.shape[axis] // 2
            a, b = lax.slice_in_dim(p, 0, n, axis=axis), lax.slice_in_dim(p, n, 2 * n, axis=axis)
            if upper:
                a = a + part.astype(F32)
            else:
                b = b + part.astype(F32)
            return jnp.concatenate([a, b], axis=axis).astype(BF16)

        def upper(self, k):
            return self.copy(self.s1.at[(k, *self.up)], self.ra.at[k], 4 * k, sn)

        def lower(self, k):
            return self.copy(self.s1.at[(k, *self.lo)], self.rb.at[k], 4 * k + 1, sp)

        def ahead(self, k):
            return self.copy(self.s2p.at[k], self.rm.at[k], 4 * k + 2, sn)

        def back(self, k):
            return self.copy(self.s2m.at[k], self.rp.at[k], 4 * k + 3, sp)

        def last(self):
            return [
                self.copy(self.s3.at[(0, *self.up)], self.fa, 16, fn),
                self.copy(self.s3.at[(0, *self.lo)], self.fb, 17, fp),
                self.copy(self.s3.at[1], self.gm, 18, fn),
                self.copy(self.s3.at[2], self.gp, 19, fp),
            ]

        def first_hop(self):
            @pl.loop(0, 4)
            def _(j):
                k = 3 - j
                self.s1[k] = self.term(k, 3).astype(BF16)
                self.upper(k).start()
                self.lower(k).start()

        def second_hop(self):
            @pl.loop(0, 4)
            def _(j):
                k = 3 - j
                p = self.term(k, 1)
                self.upper(k).wait_recv()
                self.s2p[k] = self.merge(p, self.ra[k], True)
                self.ahead(k).start()
                p = self.term(k, 2)
                self.lower(k).wait_recv()
                self.s2m[k] = self.merge(p, self.rb[k], False)
                self.back(k).start()

        def gathered(self, k):
            p = self.term(k, 0)
            self.ahead(k).wait_recv()
            self.back(k).wait_recv()
            return p + self.rm[k].astype(F32) + self.rp[k].astype(F32)

        def third_hop(self):
            c1, c2, c3, c4 = self.last()
            self.s3[0] = self.gathered(3).astype(BF16)
            c1.start()
            c2.start()
            p = self.gathered(1)
            c1.wait_recv()
            self.s3[1] = self.merge(p, self.fa[...], True)
            c3.start()
            p = self.gathered(2)
            c2.wait_recv()
            self.s3[2] = self.merge(p, self.fb[...], False)
            c4.start()

        def result(self):
            _, _, c3, c4 = self.last()
            p = self.gathered(0)
            c3.wait_recv()
            c4.wait_recv()
            return p + self.gm[...].astype(F32) + self.gp[...].astype(F32)

        def drain(self):
            for k in range(4):
                for c in (self.upper(k), self.lower(k), self.ahead(k), self.back(k)):
                    c.wait_send()
            for c in self.last():
                c.wait_send()

    sc0, sc1 = Scatter(rs0, att0, T0, 0), Scatter(rs1, att1, T1 + DEC, 1)

    def group_copies(j):
        there = (g + j) % 8
        dev = (there, t)
        return (
            pltpu.make_async_remote_copy(pack.at[j], pool.at[j], grp_send.at[0, j], grp_recv.at[0, j],
                                         device_id=dev, device_id_type=MESH),
            pltpu.make_async_remote_copy(cnt_s.at[there], cnt_r.at[j], grp_send.at[1, j], grp_recv.at[1, j],
                                         device_id=dev, device_id_type=MESH),
        )

    def send_pages():
        @pl.loop(0, 8)
        def _(j):
            there = (g + j) % 8
            want = lax.broadcasted_iota(jnp.int32, (128, 512), 0) + there * 128
            hot = jnp.where(tok_slot[0:1, :] == want, 1.0, 0.0).astype(BF16)
            pages = mm(hot, kv[...]).astype(BF16)

            @pl.when(j == 0)
            def _():
                pool[0] = pages
                cnt_r[0] = cnt_s[there]

            @pl.when(j > 0)
            def _():
                pack[j] = pages
                for c in group_copies(j):
                    c.start()

    def decode_rows():
        @pl.loop(1, 8)
        def _(j):
            for c in group_copies(j):
                c.wait_recv()

        qa = by_head(q0)
        scores, weight = [], []
        for src in range(8):
            sc = nt(qa, pool[src, :, 0:HD]) * scale
            slot = lax.broadcasted_iota(jnp.int32, (16, HD), 1) // 16
            at = pl.multiple_of((g + 8 - src) % 8 * HD, HD)
            m16 = jnp.where(slot.astype(F32) < cnt_r[src, 0:1], mult[:, pl.ds(at, HD)], 0.0)
            m = jnp.concatenate([m16[0:8], m16[0:8], m16[8:16], m16[8:16]] * 4, axis=0)
            weight.append(m)
            scores.append(jnp.where(m > 0.0, sc, NEG_FILL))
        new = jnp.concatenate([kvd[...], jnp.zeros((HD - DEC, 2 * HD), BF16)], axis=0)
        col = lax.broadcasted_iota(jnp.int32, (HD, HD), 1)
        same = (col // 16 * 8 + col % 8 == query_row((HD, HD))) & (col < DEC)
        step = lax.broadcasted_iota(jnp.int32, (HD, HD), 0) // 8 % 2
        ok = same & (col // 8 % 2 <= step)
        scores.append(jnp.where(ok, nt(qa, new[:, 0:HD]) * scale, NEG_FILL))
        top = m_c[...]
        for sc in scores:
            top = jnp.maximum(top, jnp.max(sc, axis=1, keepdims=True))
        o_swap.wait_recv()
        old = jnp.exp(m_c[...] - top)
        total = l_c[...] * old
        mixed = (o8[0:HD] + ox[...]) * old
        for i in range(9):
            e = jnp.exp(scores[i] - top)
            if i < 8:
                e = e * weight[i]
            total = total + jnp.sum(e, axis=1, keepdims=True)
            values = pool[i, :, HD:2 * HD] if i < 8 else new[:, HD:2 * HD]
            mixed = mixed + mm(e.astype(BF16), values)
        mixed = (mixed / total).astype(BF16)
        for h in range(4):
            att1[T1:T1 + DEC, h * HD:(h + 1) * HD] = mixed[h * DEC:(h + 1) * DEC]

    finish(acc0, ss0, kvs0, q0, 0, C0)
    kv_join[0].start()
    finish_q(acc0, ss0, q0, 0, C0)
    q_swap.start()
    advance(1, 9, 10, 11)
    pass_keys(0, kvs0, kvr0, 0, C0)
    cache_scores()
    for h in range(4):
        attend(q0, DEC, T0, att0, h, T0)
    loads[2].wait()
    sc0.first_hop()
    advance(1, 12, 13)
    cache_weights()
    advance(1, 14)
    cache_values()
    advance(1, 15)
    finish(acc1, ss1, kvs1, q1, C0, C1)
    kv_join[1].start()
    finish_q(acc1, ss1, q1, C0, C1)
    sc0.second_hop()
    pass_keys(1, kvs1, kvr1, C0, C1)
    send_pages()
    for h in range(4):
        attend(q1, 0, T1, att1, h, 512)
    sc0.third_hop()
    decode_rows()
    sc1.first_hop()
    sc1.second_hop()
    pre_out[0:T0] = (sc0.result() + pre_in[0:T0].astype(F32)).astype(BF16)
    sc1.third_hop()
    last = sc1.result()
    pre_out[T0:512] = (last[0:T1] + pre_in[T0:512].astype(F32)).astype(BF16)
    dsum = last[T1:T1 + DEC]
    dsum = jnp.concatenate([dsum[0:8], dsum[16:24], dsum[8:16], dsum[24:32]], axis=0)
    dec_out[...] = (dsum + dec_in[...].astype(F32)).astype(BF16)

    ag0.drain()
    ag1.drain()
    sc0.drain()
    sc1.drain()
    for c in kv_join + [q_swap, s_swap, e_swap, o_swap]:
        c.wait_send()

    @pl.loop(1, 8)
    def _(j):
        for c in group_copies(j):
            c.wait_send()


def scatter_bufs(rows):
    h, w = rows // 2, FS
    return (
        pltpu.VMEM((4, rows, FS), BF16),
        pltpu.VMEM((4, h, w), BF16),
        pltpu.VMEM((4, h, w), BF16),
        pltpu.VMEM((4, rows, FS), BF16),
        pltpu.VMEM((4, rows, FS), BF16),
        pltpu.VMEM((4, rows, FS), BF16),
        pltpu.VMEM((4, rows, FS), BF16),
        pltpu.VMEM((3, rows, FS), BF16),
        pltpu.VMEM((h, w), BF16),
        pltpu.VMEM((h, w), BF16),
        pltpu.VMEM((rows, FS), BF16),
        pltpu.VMEM((rows, FS), BF16),
    )


def body(
    prefill_in, decode_in, norm_gain, query_weight, query_bias, keyval_weight, keyval_bias,
    out_weight, pass_offset, routing, cache_len, page_table, cache_keyval,
):
    half_lanes = np.arange(HD) % 64
    freq = jnp.asarray((1000000.0 ** (-(half_lanes * (2.0 / HD)))).astype(np.float32).reshape(1, HD))
    vmem = pl.BlockSpec(memory_space=pltpu.VMEM)
    smem = pl.BlockSpec(memory_space=pltpu.SMEM)
    hbm = pl.BlockSpec(memory_space=pl.ANY)
    pre, dec = pl.pallas_call(
        kernel,
        out_shape=(
            jax.ShapeDtypeStruct((512, FS), BF16),
            jax.ShapeDtypeStruct((DEC, FS), BF16),
        ),
        in_specs=[vmem] * 6 + [smem] * 4 + [hbm] * 4,
        out_specs=(vmem, vmem),
        scratch_shapes=[
            pltpu.VMEM((18, FS), F32),
            pltpu.VMEM((16, 2, C0 // 2, FS), BF16),
            pltpu.VMEM((16, 2, C1 // 2, FS), BF16),
            pltpu.VMEM((WIDTH, FS), BF16),
            pltpu.VMEM((HD, WIDTH), BF16),
            pltpu.VMEM((FS, WIDTH), BF16),
            pltpu.VMEM((C0, 640), F32),
            pltpu.VMEM((C1, 640), F32),
            pltpu.VMEM((C0, HD), F32),
            pltpu.VMEM((C1, HD), F32),
            pltpu.VMEM((C0 + C1, HD), F32),
            pltpu.VMEM((C0 + C1, HD), F32),
            pltpu.VMEM((C0, FS), BF16),
            pltpu.VMEM((C1, FS), BF16),
            pltpu.VMEM((C0, HD), BF16),
            pltpu.VMEM((C1, HD), BF16),
            pltpu.VMEM((C0, HD), BF16),
            pltpu.VMEM((C1, HD), BF16),
            pltpu.VMEM((512, 2 * HD), BF16),
            pltpu.VMEM((DEC, 2 * HD), BF16),
            pltpu.VMEM((T0, FS), BF16),
            pltpu.VMEM((T1 + DEC, FS), BF16),
            pltpu.VMEM((16, 2, 64, CACHE), BF16),
            pltpu.VMEM((256, CACHE), F32),
            pltpu.VMEM((HD, CACHE), F32),
            pltpu.VMEM((HD, CACHE), BF16),
            pltpu.VMEM((HD, CACHE), BF16),
            pltpu.VMEM((256, HD), F32),
            pltpu.VMEM((HD, HD), F32),
            pltpu.VMEM((HD, HD), F32),
            pltpu.VMEM((HD, HD), F32),
            pltpu.VMEM((8, HD, 2 * HD), BF16),
            pltpu.VMEM((8, HD, 2 * HD), BF16),
            pltpu.VMEM((8, 8, HD), F32),
            pltpu.VMEM((8, 8, HD), F32),
            pltpu.VMEM((DEC, FS), BF16),
            pltpu.VMEM((16, 1024), F32),
            pltpu.VMEM((8, 512), jnp.int32),
            scatter_bufs(T0),
            scatter_bufs(T1 + DEC),
            pltpu.SemaphoreType.DMA((4,)),
            pltpu.SemaphoreType.DMA((2, 20)),
            pltpu.SemaphoreType.DMA((2, 20)),
            pltpu.SemaphoreType.DMA((3, 20)),
            pltpu.SemaphoreType.DMA((3, 20)),
            pltpu.SemaphoreType.DMA((6,)),
            pltpu.SemaphoreType.DMA((6,)),
            pltpu.SemaphoreType.DMA((2, 8)),
            pltpu.SemaphoreType.DMA((2, 8)),
        ],
        compiler_params=pltpu.CompilerParams(
            collective_id=0, has_side_effects=True, vmem_limit_bytes=62 * 2**20
        ),
    )(
        prefill_in,
        decode_in.reshape(DEC, FS),
        norm_gain,
        query_bias,
        keyval_bias,
        freq,
        pass_offset,
        routing.reshape(32),
        cache_len,
        page_table.T,
        query_weight,
        keyval_weight.transpose(1, 2, 0).reshape(HD, WIDTH),
        out_weight,
        cache_keyval.transpose(0, 2, 3, 1),
    )
    return pre, dec.reshape(2, 16, FS)


def solution(mesh):
    in_specs = (
        P("group", "tp"),
        P(None, "group", "tp"),
        P(),
        P(None, "tp"),
        P("tp"),
        P(None, None, "tp"),
        P(None, "tp"),
        P("tp", None),
        P("group"),
        P("group", None),
        P("group"),
        P("group", None),
        P("group", None, None, "tp"),
    )
    out_specs = (P("group", "tp"), P(None, "group", "tp"))
    return jax.shard_map(body, mesh=mesh, in_specs=in_specs, out_specs=out_specs, check_vma=False)
```

```python
import jax
import jax.numpy as jnp
import numpy as np
from jax import lax
from jax.experimental import pallas as pl
from jax.experimental.pallas import tpu as pltpu
from jax.sharding import PartitionSpec as P

MESH = pl.DeviceIdType.MESH
F32 = jnp.float32
BF16 = jnp.bfloat16
HD = 128
FS = 512
DEC = 32
T0, T1 = 256, 256
C0, C1 = DEC + T0, T1
NEG_FILL = -1e30
EPSILON = 1e-06
CACHE = 256
WIDTH = 8192


def nt(a, b):
    return lax.dot_general(a, b, (((1,), (1,)), ((), ())), preferred_element_type=F32)


def mm(a, b):
    return jnp.dot(a, b, preferred_element_type=F32)


def offset_of(k):
    return k + k // 2 - 2 * (k // 3)


def kernel(
    pre_in, dec_in, gain, qbias, kvbias, freq, offset, routing, lens, table,
    wq_hbm, wkv_hbm, wo_hbm, cache_hbm,
    pre_out, dec_out,
    params, x0, x1, wq, wkv, wo, acc0, acc1, ss0, ss1, cos_t, sin_t,
    q0, q1, kvs0, kvs1, kvr0, kvr1, kv, kvd, att0, att1,
    cache, s8, sx, e_own, ex, o8, ox, m_c, l_c, pack, pool, cnt_s, cnt_r, qx, mult,
    tok_slot,
    rs0, rs1,
    w_sem, ag_send, ag_recv, rs_send, rs_recv, pair_send, pair_recv, grp_send, grp_recv,
):
    g = lax.axis_index("group")
    t = lax.axis_index("tp")
    core = g % 2
    y, z = t // 4, t % 4
    f = z + core * (y - z)
    s = y + core * (z - y)

    def tp_of(ff, ss):
        return 4 * ss + ff + core * 3 * (ff - ss)

    fn, fp = tp_of((f + 1) % 4, s), tp_of((f + 3) % 4, s)
    sn, sp = tp_of(f, (s + 1) % 4), tp_of(f, (s + 3) % 4)
    pair = t + 1 - 2 * (t % 2)
    half = t % 2

    drows = dec_in[...].astype(F32)
    drows = jnp.concatenate([drows[0:8], drows[16:24], drows[8:16], drows[24:32]], axis=0)
    first = jnp.concatenate([drows.astype(BF16), pre_in[0:T0]], axis=0)
    x0[0] = first.reshape(2, C0 // 2, FS)
    x1[0] = pre_in[T0:512].reshape(2, C1 // 2, FS)

    barrier = pltpu.get_barrier_semaphore()
    for peer in (fn, fp, sn, sp):
        pl.semaphore_signal(barrier, inc=1, device_id=(g, peer), device_id_type=MESH)
    for j in range(1, 8):
        pl.semaphore_signal(barrier, inc=1, device_id=((g + j) % 8, t), device_id_type=MESH)

    loads = [
        pltpu.make_async_copy(wq_hbm, wq, w_sem.at[0]),
        pltpu.make_async_copy(wkv_hbm, wkv, w_sem.at[1]),
        pltpu.make_async_copy(wo_hbm, wo, w_sem.at[2]),
        pltpu.make_async_copy(cache_hbm, cache, w_sem.at[3]),
    ]
    for load in loads:
        load.start()

    pl.semaphore_wait(barrier, 11)

    def to_tp(src, dst, send, recv, peer):
        return pltpu.make_async_remote_copy(src, dst, send, recv, device_id=(g, peer), device_id_type=MESH)

    class Gather:
        def __init__(self, x, rows, c):
            self.x, self.c, self.sent = x, c, []

        def copy(self, src, dst, part, index, peer):
            src, dst = 4 * src[0] + src[1], 4 * dst[0] + dst[1]
            src = self.x.at[src] if part is None else self.x.at[src, part]
            dst = self.x.at[dst] if part is None else self.x.at[dst, part]
            return to_tp(src, dst, ag_send.at[self.c, index], ag_recv.at[self.c, index], peer)

        def go(self, src, dst, part, index, peer):
            copy = self.copy(src, dst, part, index, peer)
            copy.start()
            self.sent.append(copy)

        def came(self, dst, part, index):
            self.copy(dst, dst, part, index, fn).wait_recv()

        def send_own(self):
            self.go((0, 0), (2, 0), None, 0, fn)
            self.go((0, 0), (1, 0), None, 1, fp)
            self.line(0)

        def line(self, k):
            self.go((k, 0), (k, 2), None, 4 + 4 * k, sn)
            self.go((k, 0), (k, 1), None, 5 + 4 * k, sp)

        def near(self):
            self.came((2, 0), None, 0)
            self.go((2, 0), (3, 0), 0, 2, fn)
            self.line(2)
            self.came((1, 0), None, 1)
            self.go((1, 0), (3, 0), 1, 3, fp)
            self.line(1)

        def far(self):
            self.came((3, 0), 0, 2)
            self.came((3, 0), 1, 3)
            self.line(3)

        def step(self, i):
            j, w = (i - 3) // 3, (i - 3) % 3
            if i < 3:
                if i == 1:
                    self.near()
                return i, 0
            if i == 5:
                self.far()
                return 3, 0
            if i == 15 or w == 2:
                self.came((j - 1, 3), 0, 2 + 4 * j)
                self.came((j - 1, 3), 1, 3 + 4 * j)
                return j - 1, 3
            if w == 0:
                self.came((j, 2), None, 4 + 4 * j)
                self.go((j, 2), (j, 3), 0, 6 + 4 * j, sn)
                return j, 2
            self.came((j, 1), None, 5 + 4 * j)
            self.go((j, 1), (j, 3), 1, 7 + 4 * j, sp)
            return j, 1

        def drain(self):
            for copy in self.sent:
                copy.wait_send()

    ag0, ag1 = Gather(x0, C0, 0), Gather(x1, C1, 1)
    ag0.send_own()
    ag1.send_own()

    def accumulate(x, acc, ss, place):
        kf, ks = place
        slot = tp_of((f + offset_of(kf)) % 4, (s + offset_of(ks)) % 4)
        at = pl.multiple_of(slot * FS, FS)
        xf = x[4 * kf + ks].reshape(-1, FS).astype(F32)
        sq = xf * xf
        ss[...] += sq[:, 0:128] + sq[:, 128:256] + sq[:, 256:384] + sq[:, 384:512]
        xg = (xf * params[pl.ds(slot, 1), :]).astype(BF16)
        acc[:, 0:512] += mm(xg, wq[pl.ds(at, FS), :])
        acc[:, 512:640] += nt(xg, wkv[:, pl.ds(at, FS)])

    for i in range(16):
        params[i:i + 1] = gain[i * FS:(i + 1) * FS].astype(F32).reshape(1, FS)
    params[16:17] = qbias[...].astype(F32).reshape(1, FS)
    params[17:18, 0:HD] = jnp.concatenate([kvbias[0:1].astype(F32), kvbias[1:2].astype(F32)], axis=1)
    lane = lax.broadcasted_iota(jnp.int32, (C0, HD), 1)
    row = lax.broadcasted_iota(jnp.int32, (C0, HD), 0)
    places = row - DEC + offset[0]
    for r in range(16):
        base = (r // 8) * 16 + r % 8
        places = jnp.where(row == base, lens[r], places)
        places = jnp.where(row == base + 8, lens[r] + 1, places)
    sign = jnp.where(lane < 64, -1.0, 1.0).astype(F32)
    angle = places.astype(F32) * freq[...]
    cos_t[0:C0] = jnp.cos(angle)
    sin_t[0:C0] = jnp.sin(angle) * sign
    row = lax.broadcasted_iota(jnp.int32, (C1, HD), 0)
    angle = (row + (T0 + offset[0])).astype(F32) * freq[...]
    cos_t[C0:C0 + C1] = jnp.cos(angle)
    sin_t[C0:C0 + C1] = jnp.sin(angle) * sign[0:1]

    acc0[...] = jnp.zeros_like(acc0)
    acc1[...] = jnp.zeros_like(acc1)
    ss0[...] = jnp.zeros_like(ss0)
    ss1[...] = jnp.zeros_like(ss1)
    loads[0].wait()
    loads[1].wait()

    gathers = ((ag0, x0, acc0, ss0), (ag1, x1, acc1, ss1))

    def advance(c, *steps):
        ag, x, acc, ss = gathers[c]
        for place in [ag.step(i) for i in steps]:
            accumulate(x, acc, ss, place)

    advance(0, 0, 1, 2, 3, 4)
    advance(0, 5)

    advance(1, 0, 1, 2, 3, 4)
    advance(0, 6, 7, 8)
    advance(1, 5)
    advance(0, 9, 10, 11)
    advance(1, 6, 7, 8)
    advance(0, 12, 13)
    advance(0, 14, 15)

    def finish(acc, ss, kvs, q, table_at, rows):
        inv = lax.rsqrt(jnp.sum(ss[...], axis=1, keepdims=True) * (1.0 / WIDTH) + EPSILON)
        kvs[...] = (acc[:, 512:640] * inv + params[17:18, 0:HD]).astype(BF16)
        return inv

    def finish_q(acc, ss, q, table_at, rows):
        inv = lax.rsqrt(jnp.sum(ss[...], axis=1, keepdims=True) * (1.0 / WIDTH) + EPSILON)
        c, sn_ = cos_t[table_at:table_at + rows], sin_t[table_at:table_at + rows]
        for h in range(4):
            at = slice(h * HD, (h + 1) * HD)
            v = acc[:, at] * inv + params[16:17, at]
            q[:, at] = (v * c + pltpu.roll(v, 64, 1) * sn_).astype(BF16)

    def join(own, other, table_at, rows):
        a, b = own[...].astype(F32), other[...].astype(F32)
        lo = jnp.where(half == 0, a, b)
        hi = jnp.where(half == 0, b, a)
        low = lax.broadcasted_iota(jnp.int32, (rows, HD), 1) < 64
        k = jnp.where(low, lo, pltpu.roll(hi, 64, 1))
        v = jnp.where(low, pltpu.roll(lo, 64, 1), hi)
        k = k * cos_t[table_at:table_at + rows] + pltpu.roll(k, 64, 1) * sin_t[table_at:table_at + rows]
        return k.astype(BF16), v.astype(BF16)

    def pair_copy(src, dst, index):
        return to_tp(src, dst, pair_send.at[index], pair_recv.at[index], pair)

    kv_join = [pair_copy(kvs0, kvr0, 0), pair_copy(kvs1, kvr1, 1)]
    q_swap = pair_copy(q0.at[pl.ds(0, DEC)], qx, 2)
    s_swap = pair_copy(s8.at[pl.ds(HD, HD)], sx, 3)
    e_swap = pair_copy(e_own, ex, 4)
    o_swap = pair_copy(o8.at[pl.ds(HD, HD)], ox, 5)

    scale = HD ** (-0.5)

    def attend(q, start, rows, att, h, keys):
        at = pl.ds(h * HD, HD)
        sc = nt(q[start:start + rows, at], kv[0:keys, 0:HD]) * scale
        qi = lax.broadcasted_iota(jnp.int32, (rows, keys), 0) + (keys - rows)
        ki = lax.broadcasted_iota(jnp.int32, (rows, keys), 1)
        sc = jnp.where(ki <= qi, sc, NEG_FILL)
        e = jnp.exp(sc - jnp.max(sc, axis=1, keepdims=True))
        total = jnp.sum(e, axis=1, keepdims=True)
        att[0:rows, at] = (mm(e.astype(BF16), kv[0:keys, HD:2 * HD]) / total).astype(BF16)

    def query_row(shape):
        m = lax.broadcasted_iota(jnp.int32, shape, 0)
        return m % DEC // 16 * 8 + m % 8

    def by_head(ref):
        return jnp.concatenate([ref[0:DEC, h * HD:(h + 1) * HD] for h in range(4)], axis=0)

    def padded(part):
        zero = jnp.zeros((64, CACHE), BF16)
        return jnp.where(half == 0, jnp.concatenate([part, zero], axis=0), jnp.concatenate([zero, part], axis=0))

    def cache_scores():
        q_swap.wait_recv()
        loads[3].wait()
        q8 = jnp.concatenate([by_head(q0), by_head(qx)], axis=0)
        s8[...] = jnp.zeros_like(s8)

        @pl.loop(0, 16)
        def _(r):
            s8[...] = jnp.where(query_row((256, CACHE)) == r, mm(q8, padded(cache[r, 0])), s8[...])

        s_swap.start()

    def cache_weights():
        s_swap.wait_recv()
        owner = query_row((HD, CACHE))
        length = jnp.zeros((HD, CACHE), jnp.int32)
        for r in range(16):
            length = jnp.where(owner == r, lens[r], length)
        sc = (s8[0:HD] + sx[...]) * scale
        sc = jnp.where(lax.broadcasted_iota(jnp.int32, (HD, CACHE), 1) < length, sc, NEG_FILL)
        top = jnp.max(sc, axis=1, keepdims=True)
        e = jnp.exp(sc - top)
        m_c[...] = jnp.broadcast_to(top, (HD, HD))
        l_c[...] = jnp.broadcast_to(jnp.sum(e, axis=1, keepdims=True), (HD, HD))
        e_own[...] = e.astype(BF16)
        e_swap.start()

    def cache_values():
        e_swap.wait_recv()
        e8 = jnp.concatenate([e_own[...], ex[...]], axis=0)
        o8[...] = jnp.zeros_like(o8)

        @pl.loop(0, 16)
        def _(r):
            o8[...] = jnp.where(query_row((256, HD)) == r, nt(e8, padded(cache[r, 1])), o8[...])

        o_swap.start()

    def pass_keys(c, kvs, kvr, at, rows):
        kv_join[c].wait_recv()
        k, v = join(kvs, kvr, at, rows)
        if c == 0:
            kvd[:, 0:HD] = k[0:DEC]
            kvd[:, HD:2 * HD] = v[0:DEC]
            k, v = k[DEC:C0], v[DEC:C0]
        tokens = slice(0, T0) if c == 0 else slice(T0, 512)
        kv[tokens, 0:HD] = k
        kv[tokens, HD:2 * HD] = v

    class Scatter:
        def __init__(self, bufs, att, rows, c):
            (self.s1, self.ra, self.rb, self.s2p, self.s2m, self.rm, self.rp,
             self.s3, self.fa, self.fb, self.gm, self.gp) = bufs
            self.att, self.c = att, c
            self.up = (pl.ds(0, rows // 2), slice(None))
            self.lo = (pl.ds(rows // 2, rows // 2), slice(None))

        def term(self, kf, ks):
            slot = tp_of((f + offset_of(kf)) % 4, (s + offset_of(ks)) % 4)
            return mm(self.att[...], wo[:, pl.ds(pl.multiple_of(slot * FS, FS), FS)])

        def copy(self, src, dst, index, peer):
            return to_tp(src, dst, rs_send.at[self.c, index], rs_recv.at[self.c, index], peer)

        def merge(self, p, part, upper):
            axis = 0
            n = p.shape[axis] // 2
            a, b = lax.slice_in_dim(p, 0, n, axis=axis), lax.slice_in_dim(p, n, 2 * n, axis=axis)
            if upper:
                a = a + part.astype(F32)
            else:
                b = b + part.astype(F32)
            return jnp.concatenate([a, b], axis=axis).astype(BF16)

        def upper(self, k):
            return self.copy(self.s1.at[(k, *self.up)], self.ra.at[k], 4 * k, sn)

        def lower(self, k):
            return self.copy(self.s1.at[(k, *self.lo)], self.rb.at[k], 4 * k + 1, sp)

        def ahead(self, k):
            return self.copy(self.s2p.at[k], self.rm.at[k], 4 * k + 2, sn)

        def back(self, k):
            return self.copy(self.s2m.at[k], self.rp.at[k], 4 * k + 3, sp)

        def last(self):
            return [
                self.copy(self.s3.at[(0, *self.up)], self.fa, 16, fn),
                self.copy(self.s3.at[(0, *self.lo)], self.fb, 17, fp),
                self.copy(self.s3.at[1], self.gm, 18, fn),
                self.copy(self.s3.at[2], self.gp, 19, fp),
            ]

        def first_hop(self):
            @pl.loop(0, 4)
            def _(j):
                k = 3 - j
                self.s1[k] = self.term(k, 3).astype(BF16)
                self.upper(k).start()
                self.lower(k).start()

        def second_hop(self):
            @pl.loop(0, 4)
            def _(j):
                k = 3 - j
                p = self.term(k, 1)
                self.upper(k).wait_recv()
                self.s2p[k] = self.merge(p, self.ra[k], True)
                self.ahead(k).start()
                p = self.term(k, 2)
                self.lower(k).wait_recv()
                self.s2m[k] = self.merge(p, self.rb[k], False)
                self.back(k).start()

        def gathered(self, k):
            p = self.term(k, 0)
            self.ahead(k).wait_recv()
            self.back(k).wait_recv()
            return p + self.rm[k].astype(F32) + self.rp[k].astype(F32)

        def third_hop(self):
            c1, c2, c3, c4 = self.last()
            self.s3[0] = self.gathered(3).astype(BF16)
            c1.start()
            c2.start()
            p = self.gathered(1)
            c1.wait_recv()
            self.s3[1] = self.merge(p, self.fa[...], True)
            c3.start()
            p = self.gathered(2)
            c2.wait_recv()
            self.s3[2] = self.merge(p, self.fb[...], False)
            c4.start()

        def result(self):
            _, _, c3, c4 = self.last()
            p = self.gathered(0)
            c3.wait_recv()
            c4.wait_recv()
            return p + self.gm[...].astype(F32) + self.gp[...].astype(F32)

        def drain(self):
            for k in range(4):
                for c in (self.upper(k), self.lower(k), self.ahead(k), self.back(k)):
                    c.wait_send()
            for c in self.last():
                c.wait_send()

    sc0, sc1 = Scatter(rs0, att0, T0, 0), Scatter(rs1, att1, T1 + DEC, 1)

    def group_copies(j):
        there = (g + j) % 8
        dev = (there, t)
        return (
            pltpu.make_async_remote_copy(pack.at[j], pool.at[j], grp_send.at[0, j], grp_recv.at[0, j],
                                         device_id=dev, device_id_type=MESH),
            pltpu.make_async_remote_copy(cnt_s.at[there], cnt_r.at[j], grp_send.at[1, j], grp_recv.at[1, j],
                                         device_id=dev, device_id_type=MESH),
        )

    def send_pages():
        @pl.loop(0, 8)
        def _(j):
            there = (g + j) % 8
            want = lax.broadcasted_iota(jnp.int32, (128, 512), 0) + there * 128
            hot = jnp.where(tok_slot[0:1, :] == want, 1.0, 0.0).astype(BF16)
            pages = mm(hot, kv[...]).astype(BF16)

            @pl.when(j == 0)
            def _():
                pool[0] = pages
                cnt_r[0] = cnt_s[there]

            @pl.when(j > 0)
            def _():
                pack[j] = pages
                for c in group_copies(j):
                    c.start()

    def decode_rows():
        @pl.loop(1, 8)
        def _(j):
            for c in group_copies(j):
                c.wait_recv()

        qa = by_head(q0)
        scores, weight = [], []
        for src in range(8):
            sc = nt(qa, pool[src, :, 0:HD]) * scale
            slot = lax.broadcasted_iota(jnp.int32, (16, HD), 1) // 16
            at = pl.multiple_of((g + 8 - src) % 8 * HD, HD)
            m16 = jnp.where(slot.astype(F32) < cnt_r[src, 0:1], mult[:, pl.ds(at, HD)], 0.0)
            m = jnp.concatenate([m16[0:8], m16[0:8], m16[8:16], m16[8:16]] * 4, axis=0)
            weight.append(m)
            scores.append(jnp.where(m > 0.0, sc, NEG_FILL))
        new = jnp.concatenate([kvd[...], jnp.zeros((HD - DEC, 2 * HD), BF16)], axis=0)
        col = lax.broadcasted_iota(jnp.int32, (HD, HD), 1)
        same = (col // 16 * 8 + col % 8 == query_row((HD, HD))) & (col < DEC)
        step = lax.broadcasted_iota(jnp.int32, (HD, HD), 0) // 8 % 2
        ok = same & (col // 8 % 2 <= step)
        scores.append(jnp.where(ok, nt(qa, new[:, 0:HD]) * scale, NEG_FILL))
        top = m_c[...]
        for sc in scores:
            top = jnp.maximum(top, jnp.max(sc, axis=1, keepdims=True))
        o_swap.wait_recv()
        old = jnp.exp(m_c[...] - top)
        total = l_c[...] * old
        mixed = (o8[0:HD] + ox[...]) * old
        for i in range(9):
            e = jnp.exp(scores[i] - top)
            if i < 8:
                e = e * weight[i]
            total = total + jnp.sum(e, axis=1, keepdims=True)
            values = pool[i, :, HD:2 * HD] if i < 8 else new[:, HD:2 * HD]
            mixed = mixed + mm(e.astype(BF16), values)
        mixed = (mixed / total).astype(BF16)
        for h in range(4):
            att1[T1:T1 + DEC, h * HD:(h + 1) * HD] = mixed[h * DEC:(h + 1) * DEC]

    finish(acc0, ss0, kvs0, q0, 0, C0)
    kv_join[0].start()
    finish_q(acc0, ss0, q0, 0, C0)
    q_swap.start()
    advance(1, 9)
    pass_keys(0, kvs0, kvr0, 0, C0)
    for h in range(4):
        attend(q0, DEC, T0, att0, h, T0)
    loads[2].wait()
    sc0.first_hop()
    advance(1, 10, 11)
    advance(1, 12, 13)

    token = lax.broadcasted_iota(jnp.int32, (8, 512), 1)

    def rank_block(b, carry):
        slots, counts = carry
        d = routing[b]
        rank = jnp.int32(0)
        for k in range(8):
            rank = rank + jnp.where(d == k, counts[k], 0)
        slots = jnp.where(token // 16 == b, d * 128 + rank * 16 + token % 16, slots)
        return slots, tuple(counts[k] + jnp.where(d == k, 1, 0) for k in range(8))

    slots, counts = lax.fori_loop(
        0, 32, rank_block, (jnp.zeros((8, 512), jnp.int32), (jnp.int32(0),) * 8)
    )
    tok_slot[...] = slots
    for k in range(8):
        cnt_s[k] = jnp.full((8, 128), 1.0, F32) * counts[k].astype(F32)

    page = lax.broadcasted_iota(jnp.int32, (16, 1024), 1) // 16
    prow = lax.broadcasted_iota(jnp.int32, (16, 1024), 0)

    def count_pages(i, times):
        r, j = i // 8, i % 8
        return times + jnp.where((prow == r) & (page == table[j, r]), 1.0, 0.0)

    mult[...] = lax.fori_loop(0, 128, count_pages, jnp.zeros((16, 1024), F32))

    cache_scores()
    advance(1, 14, 15)
    finish(acc1, ss1, kvs1, q1, C0, C1)
    kv_join[1].start()
    cache_weights()
    finish_q(acc1, ss1, q1, C0, C1)
    sc0.second_hop()
    pass_keys(1, kvs1, kvr1, C0, C1)
    send_pages()
    cache_values()
    for h in range(4):
        attend(q1, 0, T1, att1, h, 512)
    sc0.third_hop()
    decode_rows()
    sc1.first_hop()
    sc1.second_hop()
    pre_out[0:T0] = (sc0.result() + pre_in[0:T0].astype(F32)).astype(BF16)
    sc1.third_hop()
    last = sc1.result()
    pre_out[T0:512] = (last[0:T1] + pre_in[T0:512].astype(F32)).astype(BF16)
    dsum = last[T1:T1 + DEC]
    dsum = jnp.concatenate([dsum[0:8], dsum[16:24], dsum[8:16], dsum[24:32]], axis=0)
    dec_out[...] = (dsum + dec_in[...].astype(F32)).astype(BF16)

    ag0.drain()
    ag1.drain()
    sc0.drain()
    sc1.drain()
    for c in kv_join + [q_swap, s_swap, e_swap, o_swap]:
        c.wait_send()

    @pl.loop(1, 8)
    def _(j):
        for c in group_copies(j):
            c.wait_send()


def scatter_bufs(rows):
    h, w = rows // 2, FS
    return (
        pltpu.VMEM((4, rows, FS), BF16),
        pltpu.VMEM((4, h, w), BF16),
        pltpu.VMEM((4, h, w), BF16),
        pltpu.VMEM((4, rows, FS), BF16),
        pltpu.VMEM((4, rows, FS), BF16),
        pltpu.VMEM((4, rows, FS), BF16),
        pltpu.VMEM((4, rows, FS), BF16),
        pltpu.VMEM((3, rows, FS), BF16),
        pltpu.VMEM((h, w), BF16),
        pltpu.VMEM((h, w), BF16),
        pltpu.VMEM((rows, FS), BF16),
        pltpu.VMEM((rows, FS), BF16),
    )


def body(
    prefill_in, decode_in, norm_gain, query_weight, query_bias, keyval_weight, keyval_bias,
    out_weight, pass_offset, routing, cache_len, page_table, cache_keyval,
):
    half_lanes = np.arange(HD) % 64
    freq = jnp.asarray((1000000.0 ** (-(half_lanes * (2.0 / HD)))).astype(np.float32).reshape(1, HD))
    vmem = pl.BlockSpec(memory_space=pltpu.VMEM)
    smem = pl.BlockSpec(memory_space=pltpu.SMEM)
    hbm = pl.BlockSpec(memory_space=pl.ANY)
    pre, dec = pl.pallas_call(
        kernel,
        out_shape=(
            jax.ShapeDtypeStruct((512, FS), BF16),
            jax.ShapeDtypeStruct((DEC, FS), BF16),
        ),
        in_specs=[vmem] * 6 + [smem] * 4 + [hbm] * 4,
        out_specs=(vmem, vmem),
        scratch_shapes=[
            pltpu.VMEM((18, FS), F32),
            pltpu.VMEM((16, 2, C0 // 2, FS), BF16),
            pltpu.VMEM((16, 2, C1 // 2, FS), BF16),
            pltpu.VMEM((WIDTH, FS), BF16),
            pltpu.VMEM((HD, WIDTH), BF16),
            pltpu.VMEM((FS, WIDTH), BF16),
            pltpu.VMEM((C0, 640), F32),
            pltpu.VMEM((C1, 640), F32),
            pltpu.VMEM((C0, HD), F32),
            pltpu.VMEM((C1, HD), F32),
            pltpu.VMEM((C0 + C1, HD), F32),
            pltpu.VMEM((C0 + C1, HD), F32),
            pltpu.VMEM((C0, FS), BF16),
            pltpu.VMEM((C1, FS), BF16),
            pltpu.VMEM((C0, HD), BF16),
            pltpu.VMEM((C1, HD), BF16),
            pltpu.VMEM((C0, HD), BF16),
            pltpu.VMEM((C1, HD), BF16),
            pltpu.VMEM((512, 2 * HD), BF16),
            pltpu.VMEM((DEC, 2 * HD), BF16),
            pltpu.VMEM((T0, FS), BF16),
            pltpu.VMEM((T1 + DEC, FS), BF16),
            pltpu.VMEM((16, 2, 64, CACHE), BF16),
            pltpu.VMEM((256, CACHE), F32),
            pltpu.VMEM((HD, CACHE), F32),
            pltpu.VMEM((HD, CACHE), BF16),
            pltpu.VMEM((HD, CACHE), BF16),
            pltpu.VMEM((256, HD), F32),
            pltpu.VMEM((HD, HD), F32),
            pltpu.VMEM((HD, HD), F32),
            pltpu.VMEM((HD, HD), F32),
            pltpu.VMEM((8, HD, 2 * HD), BF16),
            pltpu.VMEM((8, HD, 2 * HD), BF16),
            pltpu.VMEM((8, 8, HD), F32),
            pltpu.VMEM((8, 8, HD), F32),
            pltpu.VMEM((DEC, FS), BF16),
            pltpu.VMEM((16, 1024), F32),
            pltpu.VMEM((8, 512), jnp.int32),
            scatter_bufs(T0),
            scatter_bufs(T1 + DEC),
            pltpu.SemaphoreType.DMA((4,)),
            pltpu.SemaphoreType.DMA((2, 20)),
            pltpu.SemaphoreType.DMA((2, 20)),
            pltpu.SemaphoreType.DMA((3, 20)),
            pltpu.SemaphoreType.DMA((3, 20)),
            pltpu.SemaphoreType.DMA((6,)),
            pltpu.SemaphoreType.DMA((6,)),
            pltpu.SemaphoreType.DMA((2, 8)),
            pltpu.SemaphoreType.DMA((2, 8)),
        ],
        compiler_params=pltpu.CompilerParams(
            collective_id=0, has_side_effects=True, vmem_limit_bytes=62 * 2**20
        ),
    )(
        prefill_in,
        decode_in.reshape(DEC, FS),
        norm_gain,
        query_bias,
        keyval_bias,
        freq,
        pass_offset,
        routing.reshape(32),
        cache_len,
        page_table.T,
        query_weight,
        keyval_weight.transpose(1, 2, 0).reshape(HD, WIDTH),
        out_weight,
        cache_keyval.transpose(0, 2, 3, 1),
    )
    return pre, dec.reshape(2, 16, FS)


def solution(mesh):
    in_specs = (
        P("group", "tp"),
        P(None, "group", "tp"),
        P(),
        P(None, "tp"),
        P("tp"),
        P(None, None, "tp"),
        P(None, "tp"),
        P("tp", None),
        P("group"),
        P("group", None),
        P("group"),
        P("group", None),
        P("group", None, None, "tp"),
    )
    out_specs = (P("group", "tp"), P(None, "group", "tp"))
    return jax.shard_map(body, mesh=mesh, in_specs=in_specs, out_specs=out_specs, check_vma=False)
```
